128 devices in a mesh: layer: 4 (over z_lo, core), lon: 32 (over z_hi, y, x).
Axes of the slice: x: 4, y: 4, z: 4 (z_hi: 2, z_lo: 2; z = z_hi * 2 + z_lo), core: 2. Of those that a mesh axis runs over, the one named last changes fastest.
Arguments:
- frames: bfloat16 [2, 32, 1024, 128], P(None, None, 'lon'), may hold values from -6 to 6
- weights: bfloat16 [4, 9, 256, 512], P('layer'), may hold values from -0.125 to 0.125
- biases: float32 [4, 512], P('layer'), may hold values from -3 to 3
- hidden_init: bfloat16 [4, 32, 1024, 128], P('layer', None, 'lon'), may hold values from -3 to 3
- cell_init: float32 [4, 32, 1024, 128], P('layer', None, 'lon'), may hold values from -5 to 5
Outputs:
- hidden_seq: bfloat16 [4, 2, 32, 1024, 128], P('layer', None, None, 'lon')
- cell_final: float32 [4, 32, 1024, 128], P('layer', None, 'lon')
The draws below stay inside these ranges and needn't reach their ends.
All inputs are finite; a program needn't handle non-finite values.
Results may differ from the reference program's by a relative error of at most 0.0017.
Values may be sent and summed in bfloat16 or wider, within the bound.
A program may use at most 64 MiB of HBM per device.

```python
import jax
import jax.numpy as jnp

C = 128
GATES = 512
LAT = 32
TSTEPS = 2
LAYERS = 4
LON = 1024


def level_of(stream_key, shape, pieces, least, top_value):
    level, own = 1.0, jax.random.fold_in(stream_key, 6)
    for position, shards_of in pieces:
        steps = jnp.exp(jax.random.uniform(jax.random.fold_in(own, position), (shards_of,), jnp.float32, least / len(pieces), top_value / len(pieces)))
        level = level * jnp.repeat(steps, shape[position] // shards_of).reshape([-1 if axis == position else 1 for axis in range(len(shape))])
    return level


def normal_values(own_key, extent, width, most, shards=(), kind=jnp.bfloat16):
    loudness = level_of(own_key, extent, shards, -0.22, 0.18) if shards else 1.0
    array = jax.random.normal(own_key, extent, jnp.float32) * width * loudness
    return jnp.minimum(jnp.maximum(array, -most), most).astype(kind)


def setup_inputs(seed: int = 0) -> dict:
    splits = jax.random.split(jax.random.key(seed), 6)
    frames = normal_values(splits[0], (TSTEPS, LAT, LON, C), 1.0, 6.0, ((2, 32),))
    weights = normal_values(splits[1], (LAYERS, 9, 2 * C, GATES), (18 * C) ** -0.5, 0.125, ((0, 4),))
    biases = normal_values(splits[2], (LAYERS, GATES), 1.0, 3.0, ((0, 4),), jnp.float32)
    hidden_init = normal_values(splits[3], (LAYERS, LAT, LON, C), 0.5, 3.0, ((0, 4), (2, 32)))
    cell_init = normal_values(splits[4], (LAYERS, LAT, LON, C), 1.0, 5.0, ((0, 4), (2, 32)), jnp.float32)
    return dict(frames=frames, weights=weights, biases=biases, hidden_init=hidden_init, cell_init=cell_init)


def convolve(stacked, weight, gate_bias):
    band_rows, band_cols = stacked.shape[0], stacked.shape[1]
    padded = jnp.pad(stacked, ((0, 0), (1, 1), (0, 0)), mode="wrap")
    padded = jnp.pad(padded, ((1, 1), (0, 0), (0, 0)))
    summed = jnp.zeros((band_rows * band_cols, weight.shape[2]), jnp.float32)
    for offset in range(9):
        row_off, col_off = offset // 3, offset % 3
        window_block = padded[row_off:row_off + band_rows, col_off:col_off + band_cols].reshape(band_rows * band_cols, -1)
        summed = summed + jnp.dot(window_block, weight[offset], preferred_element_type=jnp.float32)
    return summed + gate_bias[None, :]


def gate_update(gate_sums, memory):
    chans = memory.shape[-1]
    flat_memory = memory.reshape(-1, chans)
    ingate = jax.nn.sigmoid(gate_sums[:, :chans])
    forget = jax.nn.sigmoid(gate_sums[:, chans:2 * chans])
    candidate = jnp.tanh(gate_sums[:, 2 * chans:3 * chans])
    outgate = jax.nn.sigmoid(gate_sums[:, 3 * chans:])
    new_memory = forget * flat_memory + ingate * candidate
    new_hidden = (outgate * jnp.tanh(new_memory)).astype(jnp.bfloat16)
    return new_hidden.reshape(memory.shape), new_memory.reshape(memory.shape)


def reference(frames, weights, biases, hidden_init, cell_init):
    layer_inputs = [frames[step_index] for step_index in range(TSTEPS)]
    all_hidden = []
    all_cells = []
    for layer_index in range(LAYERS):
        hidden = hidden_init[layer_index]
        memory = cell_init[layer_index]
        outputs = []
        for step_index in range(TSTEPS):
            stacked = jnp.concatenate([layer_inputs[step_index], hidden], axis=-1)
            gate_sums = convolve(stacked, weights[layer_index], biases[layer_index])
            hidden, memory = gate_update(gate_sums, memory)
            outputs.append(hidden)
        layer_inputs = outputs
        all_hidden.append(jnp.stack(outputs))
        all_cells.append(memory)
    return jnp.stack(all_hidden), jnp.stack(all_cells)
```

```python
import jax
import jax.numpy as jnp
from jax import lax
from jax.experimental import pallas as pl
from jax.experimental.pallas import tpu as pltpu
from jax.sharding import PartitionSpec as P

MESH = pl.DeviceIdType.MESH
PAD = 8
WIDTH = 48
EDGE = 5
CELL_EDGE = 4
ORDER = ((0, 0), (0, 1), (1, 0), (0, 2), (0, 3), (1, 1), (1, 2), (1, 3))


def row_shifts(columns):
    blank = jnp.zeros((columns.shape[0], 1, columns.shape[2]), columns.dtype)
    above = jnp.concatenate([blank, columns[:, :-1]], axis=1)
    below = jnp.concatenate([columns[:, 1:], blank], axis=1)
    return above, below


def gate_update(gate_sums, memory):
    chans = memory.shape[-1]
    ingate = 0.5 * jnp.tanh(0.5 * gate_sums[:, :chans]) + 0.5
    forget = 0.5 * jnp.tanh(0.5 * gate_sums[:, chans : 2 * chans]) + 0.5
    candidate = jnp.tanh(gate_sums[:, 2 * chans : 3 * chans])
    outgate = 0.5 * jnp.tanh(0.5 * gate_sums[:, 3 * chans :]) + 0.5
    new_memory = forget * memory + ingate * candidate
    return outgate * jnp.tanh(new_memory), new_memory


def kernel(
    layers, sectors,
    frames, weights, biases, hidden_init, cell_init, hidden_out, cell_out,
    w, bias, stage_h, stage_c, stage_u, hc, hs, uc, us, cells, out_h, out_c,
    load_sem, w_sem, edge_send, edge_recv, next_send, next_recv, out_sem,
):
    layer, sector = lax.axis_index("layer"), lax.axis_index("lon")
    right, left = lax.rem(sector + 1, sectors), lax.rem(sector + sectors - 1, sectors)
    steps, rows, cols, chans = stage_u.shape

    load_h = pltpu.make_async_copy(hidden_init.at[0], stage_h, load_sem.at[0])
    load_c = pltpu.make_async_copy(cell_init.at[0], stage_c, load_sem.at[1])
    load_u = [pltpu.make_async_copy(frames.at[t], stage_u.at[t], load_sem.at[2 + t]) for t in range(steps)]
    load_b = pltpu.make_async_copy(biases, bias, load_sem.at[4])
    load_w = [pltpu.make_async_copy(weights.at[0, i], w.at[i], w_sem.at[i]) for i in range(9)]
    load_h.start()

    @pl.when(layer == 0)
    def _():
        load_u[0].start()

    load_c.start()
    for copy in load_w:
        copy.start()
    load_b.start()

    @pl.when(layer == 0)
    def _():
        load_u[1].start()

    barrier = pltpu.get_barrier_semaphore()
    for side in (left, right):
        pl.semaphore_signal(barrier, inc=1, device_id=(layer, side), device_id_type=MESH)

    @pl.when(layer > 0)
    def _():
        pl.semaphore_signal(barrier, inc=1, device_id=(layer - 1, sector), device_id_type=MESH)

    def edge_copies(index, buffer, width):
        out = []
        for side, source, target, which in (
            (right, PAD + cols - width, PAD - width, 0),
            (left, PAD, PAD + cols, 1),
        ):
            out.append(
                pltpu.make_async_remote_copy(
                    src_ref=buffer.at[pl.ds(source, width)],
                    dst_ref=buffer.at[pl.ds(target, width)],
                    send_sem=edge_send.at[2 * index + which],
                    recv_sem=edge_recv.at[2 * index + which],
                    device_id=(layer, side),
                    device_id_type=MESH,
                )
            )
        return out

    edges_h = edge_copies(0, hc.at[0], EDGE)
    edges_c = edge_copies(1, cells.at[0], CELL_EDGE)
    edges_u = [edge_copies(2 + t, uc.at[t], EDGE) for t in range(steps)]

    def shift_into(center, shifted, start, count):
        above, below = row_shifts(center[pl.ds(start, count)])
        shifted[0, pl.ds(start, count)] = above
        shifted[1, pl.ds(start, count)] = below

    load_h.wait()
    hc[0, pl.ds(PAD, cols)] = jnp.swapaxes(stage_h[...], 0, 1)

    @pl.when(layer < layers - 1)
    def _():
        pl.semaphore_wait(barrier, 3)

    @pl.when(layer == layers - 1)
    def _():
        pl.semaphore_wait(barrier, 2)

    for copy in edges_h:
        copy.start()

    @pl.when(layer == 0)
    def _():
        load_u[0].wait()
        uc[0, pl.ds(PAD, cols)] = jnp.swapaxes(stage_u[0], 0, 1)
        for copy in edges_u[0]:
            copy.start()

    load_c.wait()
    cells[0, pl.ds(PAD, cols)] = jnp.swapaxes(stage_c[...], 0, 1)
    for copy in edges_c:
        copy.start()

    shift_into(hc.at[0], hs.at[0], PAD, cols)

    @pl.when(layer == 0)
    def _():
        shift_into(uc.at[0], us.at[0], PAD, cols)
        load_u[1].wait()
        uc[1, pl.ds(PAD, cols)] = jnp.swapaxes(stage_u[1], 0, 1)
        for copy in edges_u[1]:
            copy.start()
        shift_into(uc.at[1], us.at[1], PAD, cols)

    def finish_edges():
        for copy in edges_h + edges_c:
            copy.wait_recv()
        shift_into(hc.at[0], hs.at[0], PAD - EDGE, EDGE)
        shift_into(hc.at[0], hs.at[0], PAD + cols, EDGE)

        @pl.when(layer == 0)
        def _():
            for t in range(steps):
                for copy in edges_u[t]:
                    copy.wait_recv()
                shift_into(uc.at[t], us.at[t], PAD - EDGE, EDGE)
                shift_into(uc.at[t], us.at[t], PAD + cols, EDGE)

    def spans(depth, k):
        if k == 0:
            return (PAD + 8 + depth, PAD + 16 - depth), 8
        return (PAD + 8 + depth - 4 * k, PAD + 20 - depth + 4 * k), 4

    def sends(t, k, depth):
        if k == 0:
            pieces = ((PAD + 8 + depth, 16 - 2 * depth),)
        else:
            starts, count = spans(depth, k)
            pieces = tuple((start, count) for start in starts)
        return [
            pltpu.make_async_remote_copy(
                src_ref=hc.at[t + 1, pl.ds(start, count)],
                dst_ref=uc.at[t, pl.ds(start, count)],
                send_sem=next_send.at[t, k, i],
                recv_sem=next_recv.at[t, k, i],
                device_id=(layer + 1, sector),
                device_id_type=MESH,
            )
            for i, (start, count) in enumerate(pieces)
        ], pieces

    def receive(t, k):
        if k == 0:
            for source in range(layers - 1):

                @pl.when(layer == source + 1)
                def _():
                    copies, pieces = sends(t, 0, source + t)
                    copies[0].wait_recv()
                    shift_into(uc.at[t], us.at[t], *pieces[0])
        else:

            @pl.when(layer > 0)
            def _():
                copies, pieces = sends(t, k, layer - 1 + t)
                for copy, piece in zip(copies, pieces):
                    copy.wait_recv()
                    shift_into(uc.at[t], us.at[t], *piece)

    def forward(t, k, act):
        if k == 0:
            for source in range(layers - 1):

                @pl.when(layer == source)
                def _():
                    for copy in sends(t, 0, source + t)[0]:
                        act(copy)
        else:

            @pl.when(layer < layers - 1)
            def _():
                for copy in sends(t, k, layer + t)[0]:
                    act(copy)

    def compute(t, k):
        depth = layer + t
        starts, count = spans(depth, k)
        flat = count * rows

        def window(center, shifted, a, b):
            pick = {0: lambda s: shifted[0, s], 1: lambda s: center[s], 2: lambda s: shifted[1, s]}[a]
            return jnp.concatenate(
                [pick(pl.ds(start + b - 1, count)).reshape(flat, chans) for start in starts], axis=0
            )

        patches = jnp.concatenate(
            [
                part
                for a in range(3)
                for b in range(3)
                for part in (
                    window(uc.at[t], us.at[t], a, b),
                    window(hc.at[t], hs.at[t], a, b),
                )
            ],
            axis=1,
        )
        sums = jnp.dot(patches, w[...].reshape(18 * chans, 4 * chans), preferred_element_type=jnp.float32)
        sums = sums + bias[...]
        memory = jnp.concatenate([cells[t, pl.ds(start, count)].reshape(flat, chans) for start in starts], axis=0)
        hidden, memory = gate_update(sums, memory)
        hidden = hidden.astype(jnp.bfloat16).reshape(2, count, rows, chans)
        memory = memory.reshape(2, count, rows, chans)
        for i, start in enumerate(starts):
            cells[t + 1, pl.ds(start, count)] = memory[i]
            hc[t + 1, pl.ds(start, count)] = hidden[i]
        forward(t, k, lambda copy: copy.start())
        if t + 1 < steps:
            for i, start in enumerate(starts):
                above, below = row_shifts(hidden[i])
                hs[t + 1, 0, pl.ds(start, count)] = above
                hs[t + 1, 1, pl.ds(start, count)] = below

    store_h = [pltpu.make_async_copy(out_h.at[t], hidden_out.at[0, t], out_sem.at[t]) for t in range(steps)]
    store_c = pltpu.make_async_copy(out_c, cell_out.at[0], out_sem.at[steps])

    for copy in load_w:
        copy.wait()
    load_b.wait()
    for t, k in ORDER:
        if (t, k) == (0, 2):
            finish_edges()
        receive(t, k)
        compute(t, k)
        if k == 3:
            out_h[t] = jnp.swapaxes(hc[t + 1, pl.ds(PAD, cols)], 0, 1)
            store_h[t].start()
    out_c[...] = jnp.swapaxes(cells[steps, pl.ds(PAD, cols)], 0, 1)
    store_c.start()

    for copy in edges_h + edges_c:
        copy.wait_send()

    @pl.when(layer == 0)
    def _():
        for copies in edges_u:
            for copy in copies:
                copy.wait_send()

    for t, k in ORDER:
        forward(t, k, lambda copy: copy.wait_send())
    for copy in store_h + [store_c]:
        copy.wait()


def solution(mesh):
    layers, sectors = mesh.shape["layer"], mesh.shape["lon"]

    def local(frames, weights, biases, hidden_init, cell_init):
        steps, rows, cols, chans = frames.shape
        bf16, f32 = jnp.bfloat16, jnp.float32
        any_space = pl.BlockSpec(memory_space=pl.ANY)
        return pl.pallas_call(
            lambda *refs: kernel(layers, sectors, *refs),
            out_shape=[
                jax.ShapeDtypeStruct((1, steps, rows, cols, chans), bf16),
                jax.ShapeDtypeStruct((1, rows, cols, chans), f32),
            ],
            in_specs=[any_space] * 5,
            out_specs=[any_space] * 2,
            scratch_shapes=[
                pltpu.VMEM((9, 2 * chans, 4 * chans), bf16),
                pltpu.VMEM((1, 4 * chans), f32),
                pltpu.VMEM((rows, cols, chans), bf16),
                pltpu.VMEM((rows, cols, chans), f32),
                pltpu.VMEM((steps, rows, cols, chans), bf16),
                pltpu.VMEM((steps + 1, WIDTH, rows, chans), bf16),
                pltpu.VMEM((steps, 2, WIDTH, rows, chans), bf16),
                pltpu.VMEM((steps, WIDTH, rows, chans), bf16),
                pltpu.VMEM((steps, 2, WIDTH, rows, chans), bf16),
                pltpu.VMEM((steps + 1, WIDTH, rows, chans), f32),
                pltpu.VMEM((steps, rows, cols, chans), bf16),
                pltpu.VMEM((rows, cols, chans), f32),
                pltpu.SemaphoreType.DMA((5,)),
                pltpu.SemaphoreType.DMA((9,)),
                pltpu.SemaphoreType.DMA((8,)),
                pltpu.SemaphoreType.DMA((8,)),
                pltpu.SemaphoreType.DMA((steps, 4, 2)),
                pltpu.SemaphoreType.DMA((steps, 4, 2)),
                pltpu.SemaphoreType.DMA((steps + 1,)),
            ],
            compiler_params=pltpu.CompilerParams(
                collective_id=0, has_side_effects=True, vmem_limit_bytes=48 * 1024 * 1024
            ),
            name="conv_lstm",
        )(frames, weights, biases, hidden_init, cell_init)

    in_specs = (
        P(None, None, "lon", None),
        P("layer", None, None, None),
        P("layer", None),
        P("layer", None, "lon", None),
        P("layer", None, "lon", None),
    )
    out_specs = (P("layer", None, None, "lon", None), P("layer", None, "lon", None))
    return jax.shard_map(local, mesh=mesh, in_specs=in_specs, out_specs=out_specs, check_vma=False)
```

```python
import jax
import jax.numpy as jnp
from jax import lax
from jax.experimental import pallas as pl
from jax.experimental.pallas import tpu as pltpu
from jax.sharding import PartitionSpec as P

MESH = pl.DeviceIdType.MESH
PAD = 8
WIDTH = 48
EDGE = 5
CELL_EDGE = 4
ORDER = ((0, "mid"), (0, "near"), (1, "mid"), (1, "near"), (0, "east"), (1, "east"), (0, "west"), (1, "west"))
CHUNKS = ("mid", "near", "east", "west")


def spans(depth, chunk):
    if chunk == "mid":
        return (PAD + 8 + depth, PAD + 16 - depth), 8
    if chunk == "near":
        return (PAD + 1 + depth, PAD + 24 - depth), 7
    if chunk == "east":
        return (PAD + 31 - depth,), 5
    return (PAD - 4 + depth,), 5


def row_shifts(columns):
    blank = jnp.zeros((columns.shape[0], 1, columns.shape[2]), columns.dtype)
    above = jnp.concatenate([blank, columns[:, :-1]], axis=1)
    below = jnp.concatenate([columns[:, 1:], blank], axis=1)
    return above, below


def gate_update(gate_sums, memory):
    chans = memory.shape[-1]
    ingate = 0.5 * jnp.tanh(0.5 * gate_sums[:, :chans]) + 0.5
    forget = 0.5 * jnp.tanh(0.5 * gate_sums[:, chans : 2 * chans]) + 0.5
    candidate = jnp.tanh(gate_sums[:, 2 * chans : 3 * chans])
    outgate = 0.5 * jnp.tanh(0.5 * gate_sums[:, 3 * chans :]) + 0.5
    new_memory = forget * memory + ingate * candidate
    return outgate * jnp.tanh(new_memory), new_memory


def kernel(
    layers, sectors,
    frames, weights, biases, hidden_init, cell_init, h_new, cell_new,
    w, bias, stage_h, stage_c, stage_u, h_old, hs, uc, us, cell_old, cell_mid,
    load_sem, w_sem, edge_send, edge_recv, next_send, next_recv, late_sem,
):
    layer, sector = lax.axis_index("layer"), lax.axis_index("lon")
    right, left = lax.rem(sector + 1, sectors), lax.rem(sector + sectors - 1, sectors)
    steps, rows, cols, chans = stage_u.shape
    first, last = sector == 0, sector == sectors - 1
    h_at = [h_old] + [h_new.at[t] for t in range(steps)]
    cell_at = [cell_old, cell_mid, cell_new]

    load_h = pltpu.make_async_copy(hidden_init.at[0], stage_h, load_sem.at[0])
    load_c = pltpu.make_async_copy(cell_init.at[0], stage_c, load_sem.at[1])
    load_u = [pltpu.make_async_copy(frames.at[t], stage_u.at[t], load_sem.at[2 + t]) for t in range(steps)]
    load_b = pltpu.make_async_copy(biases, bias, load_sem.at[4])
    load_w = [pltpu.make_async_copy(weights.at[0, i], w.at[i], w_sem.at[i]) for i in range(9)]

    barrier = pltpu.get_barrier_semaphore()
    load_h.start()

    @pl.when(layer == 0)
    def _():
        load_u[0].start()

    pl.semaphore_signal(barrier, inc=1, device_id=(layer, left), device_id_type=MESH)

    @pl.when(jnp.logical_not(last))
    def _():
        pl.semaphore_signal(barrier, inc=1, device_id=(layer, right), device_id_type=MESH)

    @pl.when(layer > 0)
    def _():
        pl.semaphore_signal(barrier, inc=1, device_id=(layer - 1, sector), device_id_type=MESH)

    load_c.start()

    @pl.when(layer == 0)
    def _():
        load_u[1].start()

    load_b.start()
    for copy in load_w:
        copy.start()

    def edge_copies(index, buffer, width):
        return [
            pltpu.make_async_remote_copy(
                src_ref=buffer.at[pl.ds(source, width)],
                dst_ref=buffer.at[pl.ds(target, width)],
                send_sem=edge_send.at[2 * index + which],
                recv_sem=edge_recv.at[2 * index + which],
                device_id=(layer, side),
                device_id_type=MESH,
            )
            for side, source, target, which in (
                (right, PAD + cols - width, PAD - width, 0),
                (left, PAD, PAD + cols, 1),
            )
        ]

    edges_h = edge_copies(0, h_old, EDGE)
    edges_c = edge_copies(1, cell_old, CELL_EDGE)
    edges_u = [edge_copies(2 + t, uc.at[t], EDGE) for t in range(steps)]

    def send_edges(edges):
        edges[0].start()

        @pl.when(jnp.logical_not(first))
        def _():
            edges[1].start()

    def place(target, staged, start, stop):
        target[pl.ds(PAD + start, stop - start)] = jnp.swapaxes(staged[:, start:stop], 0, 1)

    def place_ends(target, staged):
        place(target, staged, 0, 8)
        place(target, staged, cols - 8, cols)

    def shift_into(center, shifted, start, count):
        above, below = row_shifts(center[pl.ds(start, count)])
        shifted[0, pl.ds(start, count)] = above
        shifted[1, pl.ds(start, count)] = below

    load_h.wait()
    place_ends(h_old, stage_h)
    awaited = 3 - (layer == layers - 1).astype(jnp.int32) - first.astype(jnp.int32)
    pl.semaphore_wait(barrier, awaited)

    @pl.when(last)
    def _():
        pl.semaphore_signal(late_sem, inc=1, device_id=(layer, right), device_id_type=MESH)

    send_edges(edges_h)

    @pl.when(layer == 0)
    def _():
        load_u[0].wait()
        place_ends(uc.at[0], stage_u.at[0])
        send_edges(edges_u[0])

    load_c.wait()
    place_ends(cell_old, stage_c)
    send_edges(edges_c)

    @pl.when(layer == 0)
    def _():
        load_u[1].wait()
        place_ends(uc.at[1], stage_u.at[1])
        send_edges(edges_u[1])

    place(h_old, stage_h, 8, cols - 8)
    place(cell_old, stage_c, 8, cols - 8)
    shift_into(h_old, hs.at[0], PAD, cols)

    @pl.when(layer == 0)
    def _():
        for t in range(steps):
            place(uc.at[t], stage_u.at[t], 8, cols - 8)
            shift_into(uc.at[t], us.at[t], PAD, cols)

    def finish_edges(which):
        start = (PAD - EDGE, PAD + cols)[which]
        edges_h[which].wait_recv()
        edges_c[which].wait_recv()
        shift_into(h_old, hs.at[0], start, EDGE)

        @pl.when(layer == 0)
        def _():
            for t in range(steps):
                edges_u[t][which].wait_recv()
                shift_into(uc.at[t], us.at[t], start, EDGE)

    def to_next(t, chunk, pieces):
        return [
            pltpu.make_async_remote_copy(
                src_ref=h_new.at[t, pl.ds(start, count)],
                dst_ref=uc.at[t, pl.ds(start, count)],
                send_sem=next_send.at[t, CHUNKS.index(chunk), i],
                recv_sem=next_recv.at[t, CHUNKS.index(chunk), i],
                device_id=(layer + 1, sector),
                device_id_type=MESH,
            )
            for i, (start, count) in enumerate(pieces)
        ]

    def each_piece(t, chunk, source, act):
        if chunk == "mid":
            for known in range(layers - 1):

                @pl.when(source == known)
                def _():
                    pieces = ((PAD + 8 + known + t, 16 - 2 * (known + t)),)
                    for copy, piece in zip(to_next(t, chunk, pieces), pieces):
                        act(copy, piece)
        else:

            @pl.when(jnp.logical_and(source >= 0, source < layers - 1))
            def _():
                starts, count = spans(source + t, chunk)
                pieces = tuple((start, count) for start in starts)
                for copy, piece in zip(to_next(t, chunk, pieces), pieces):
                    act(copy, piece)

    def receive(t, chunk):
        def act(copy, piece):
            copy.wait_recv()
            shift_into(uc.at[t], us.at[t], *piece)

        each_piece(t, chunk, layer - 1, act)

    def compute(t, chunk):
        starts, count = spans(layer + t, chunk)
        flat = count * rows

        def window(center, shifted, a, b):
            pick = (lambda s: shifted[0, s], lambda s: center[s], lambda s: shifted[1, s])[a]
            return jnp.concatenate(
                [pick(pl.ds(start + b - 1, count)).reshape(flat, chans) for start in starts], axis=0
            )

        patches = jnp.concatenate(
            [
                part
                for a in range(3)
                for b in range(3)
                for part in (
                    window(uc.at[t], us.at[t], a, b),
                    window(h_at[t], hs.at[t], a, b),
                )
            ],
            axis=1,
        )
        sums = jnp.dot(patches, w[...].reshape(18 * chans, 4 * chans), preferred_element_type=jnp.float32)
        sums = sums + bias[...]
        memory = jnp.concatenate([cell_at[t][pl.ds(start, count)].reshape(flat, chans) for start in starts], axis=0)
        hidden, memory = gate_update(sums, memory)
        hidden = hidden.astype(jnp.bfloat16).reshape(len(starts), count, rows, chans)
        memory = memory.reshape(len(starts), count, rows, chans)
        for i, start in enumerate(starts):
            h_new[t, pl.ds(start, count)] = hidden[i]
            cell_at[t + 1][pl.ds(start, count)] = memory[i]
        each_piece(t, chunk, layer, lambda copy, piece: copy.start())
        if t + 1 < steps:
            for i, start in enumerate(starts):
                above, below = row_shifts(hidden[i])
                hs[t + 1, 0, pl.ds(start, count)] = above
                hs[t + 1, 1, pl.ds(start, count)] = below

    for copy in load_w:
        copy.wait()
    load_b.wait()
    for t, chunk in ORDER:
        if (t, chunk) == (0, "east"):

            @pl.when(first)
            def _():
                pl.semaphore_wait(late_sem, 1)
                for edges in (edges_h, edges_c):
                    edges[1].start()

                @pl.when(layer == 0)
                def _():
                    for edges in edges_u:
                        edges[1].start()

            finish_edges(1)
        if (t, chunk) == (0, "west"):
            finish_edges(0)
        receive(t, chunk)
        compute(t, chunk)

    for copy in edges_h + edges_c:
        copy.wait_send()

    @pl.when(layer == 0)
    def _():
        for edges in edges_u:
            for copy in edges:
                copy.wait_send()

    for t, chunk in ORDER:
        each_piece(t, chunk, layer, lambda copy, piece: copy.wait_send())


def finish(h_ref, cell_ref, hidden_out, cell_out, out_h, out_c, sems):
    steps, rows, cols, chans = out_h.shape
    copies = []
    for t in range(steps):
        out_h[t] = jnp.swapaxes(h_ref[t, pl.ds(PAD, cols)], 0, 1)
        copies.append(pltpu.make_async_copy(out_h.at[t], hidden_out.at[0, t], sems.at[t]))
        copies[-1].start()
    out_c[...] = jnp.swapaxes(cell_ref[pl.ds(PAD, cols)], 0, 1)
    copies.append(pltpu.make_async_copy(out_c, cell_out.at[0], sems.at[steps]))
    copies[-1].start()
    for copy in copies:
        copy.wait()


def solution(mesh):
    layers, sectors = mesh.shape["layer"], mesh.shape["lon"]

    def local(frames, weights, biases, hidden_init, cell_init):
        steps, rows, cols, chans = frames.shape
        bf16, f32 = jnp.bfloat16, jnp.float32
        in_hbm = pl.BlockSpec(memory_space=pltpu.HBM)
        in_vmem = pl.BlockSpec(memory_space=pltpu.VMEM)
        operands = [
            pltpu.with_memory_space_constraint(x, pltpu.HBM)
            for x in (frames, weights, biases, hidden_init, cell_init)
        ]
        hidden, memory = pl.pallas_call(
            lambda *refs: kernel(layers, sectors, *refs),
            out_shape=[
                pltpu.VMEM((steps, WIDTH, rows, chans), bf16),
                pltpu.VMEM((WIDTH, rows, chans), f32),
            ],
            in_specs=[in_hbm] * 5,
            out_specs=[in_vmem] * 2,
            scratch_shapes=[
                pltpu.VMEM((9, 2 * chans, 4 * chans), bf16),
                pltpu.VMEM((1, 4 * chans), f32),
                pltpu.VMEM((rows, cols, chans), bf16),
                pltpu.VMEM((rows, cols, chans), f32),
                pltpu.VMEM((steps, rows, cols, chans), bf16),
                pltpu.VMEM((WIDTH, rows, chans), bf16),
                pltpu.VMEM((steps, 2, WIDTH, rows, chans), bf16),
                pltpu.VMEM((steps, WIDTH, rows, chans), bf16),
                pltpu.VMEM((steps, 2, WIDTH, rows, chans), bf16),
                pltpu.VMEM((WIDTH, rows, chans), f32),
                pltpu.VMEM((WIDTH, rows, chans), f32),
                pltpu.SemaphoreType.DMA((5,)),
                pltpu.SemaphoreType.DMA((9,)),
                pltpu.SemaphoreType.DMA((8,)),
                pltpu.SemaphoreType.DMA((8,)),
                pltpu.SemaphoreType.DMA((steps, 4, 2)),
                pltpu.SemaphoreType.DMA((steps, 4, 2)),
                pltpu.SemaphoreType.REGULAR,
            ],
            compiler_params=pltpu.CompilerParams(
                collective_id=0, has_side_effects=True, vmem_limit_bytes=40 * 1024 * 1024
            ),
            name="conv_lstm",
        )(*operands)
        hidden = pltpu.with_memory_space_constraint(hidden, pltpu.VMEM)
        memory = pltpu.with_memory_space_constraint(memory, pltpu.VMEM)
        return pl.pallas_call(
            finish,
            out_shape=[
                jax.ShapeDtypeStruct((1, steps, rows, cols, chans), bf16),
                jax.ShapeDtypeStruct((1, rows, cols, chans), f32),
            ],
            in_specs=[in_vmem] * 2,
            out_specs=[in_hbm] * 2,
            scratch_shapes=[
                pltpu.VMEM((steps, rows, cols, chans), bf16),
                pltpu.VMEM((rows, cols, chans), f32),
                pltpu.SemaphoreType.DMA((steps + 1,)),
            ],
            compiler_params=pltpu.CompilerParams(vmem_limit_bytes=16 * 1024 * 1024),
            name="write_out",
        )(hidden, memory)

    in_specs = (
        P(None, None, "lon", None),
        P("layer", None, None, None),
        P("layer", None),
        P("layer", None, "lon", None),
        P("layer", None, "lon", None),
    )
    out_specs = (P("layer", None, None, "lon", None), P("layer", None, "lon", None))
    return jax.shard_map(local, mesh=mesh, in_specs=in_specs, out_specs=out_specs, check_vma=False)
```

```python
import jax
import jax.numpy as jnp
from jax import lax
from jax.experimental import pallas as pl
from jax.experimental.pallas import tpu as pltpu
from jax.sharding import PartitionSpec as P

MESH = pl.DeviceIdType.MESH
PAD = 8
WIDTH = 48
EDGE = 5
ORDER = (
    (0, "mid"), (0, "near"), (1, "mid"), (1, "near"),
    (0, "side"), (1, "side"), (0, "other"), (1, "other"),
)
CHUNKS = ("mid", "near", "side", "other")


def row_shifts(columns):
    blank = jnp.zeros((columns.shape[0], 1, columns.shape[2]), columns.dtype)
    above = jnp.concatenate([blank, columns[:, :-1]], axis=1)
    below = jnp.concatenate([columns[:, 1:], blank], axis=1)
    return above, below


def gate_update(gate_sums, memory):
    chans = memory.shape[-1]
    ingate = 0.5 * jnp.tanh(0.5 * gate_sums[:, :chans]) + 0.5
    forget = 0.5 * jnp.tanh(0.5 * gate_sums[:, chans : 2 * chans]) + 0.5
    candidate = jnp.tanh(gate_sums[:, 2 * chans : 3 * chans])
    outgate = 0.5 * jnp.tanh(0.5 * gate_sums[:, 3 * chans :]) + 0.5
    new_memory = forget * memory + ingate * candidate
    return outgate * jnp.tanh(new_memory), new_memory


def kernel(
    layers, sectors,
    frames, weights, biases, hidden_init, cell_init, h_out, cell_out,
    w, bias, stage_h, stage_c, stage_u, h_old, h_new, hs, uc, us, cell_old, cell_mid, cell_new, partial_mid, partial_near,
    load_sem, w_sem, edge_send, edge_recv, next_send, next_recv, late_sem,
):
    layer, sector = lax.axis_index("layer"), lax.axis_index("lon")
    right, left = lax.rem(sector + 1, sectors), lax.rem(sector + sectors - 1, sectors)
    steps, rows, cols, chans = stage_u.shape
    first, last = sector == 0, sector == sectors - 1
    far = jnp.logical_or(sector == sectors // 2 - 1, sector == sectors // 2)
    h_at = [h_old] + [h_new.at[t] for t in range(steps)]
    cell_at = [cell_old, cell_mid, cell_new]
    base, upper = layer == 0, layer > 0
    flipped = jnp.logical_or(last, sector == sectors // 2 - 1)

    load_h = pltpu.make_async_copy(hidden_init.at[0], stage_h, load_sem.at[0])
    load_c = pltpu.make_async_copy(cell_init.at[0], stage_c, load_sem.at[1])
    load_u = [pltpu.make_async_copy(frames.at[t], stage_u.at[t], load_sem.at[2 + t]) for t in range(steps)]
    load_b = pltpu.make_async_copy(biases, bias, load_sem.at[4])
    load_w = [pltpu.make_async_copy(weights.at[0, i], w.at[i], w_sem.at[i]) for i in range(9)]

    barrier = pltpu.get_barrier_semaphore()
    load_h.start()

    @pl.when(base)
    def _():
        load_u[0].start()

    pl.semaphore_signal(barrier, inc=1, device_id=(layer, left), device_id_type=MESH)

    @pl.when(jnp.logical_not(last))
    def _():
        pl.semaphore_signal(barrier, inc=1, device_id=(layer, right), device_id_type=MESH)

    @pl.when(upper)
    def _():
        pl.semaphore_signal(barrier, inc=1, device_id=(layer - 1, sector), device_id_type=MESH)

    load_c.start()
    for copy in load_w:
        copy.start()
    load_b.start()

    @pl.when(base)
    def _():
        load_u[1].start()

    def edge_copies(index, buffer, width):
        return [
            pltpu.make_async_remote_copy(
                src_ref=buffer.at[pl.ds(source, width)],
                dst_ref=buffer.at[pl.ds(target, width)],
                send_sem=edge_send.at[2 * index + which],
                recv_sem=edge_recv.at[2 * index + which],
                device_id=(layer, side),
                device_id_type=MESH,
            )
            for side, source, target, which in (
                (right, PAD + cols - width, PAD - width, 0),
                (left, PAD, PAD + cols, 1),
            )
        ]

    edges_u = [edge_copies(2 + t, uc.at[t], EDGE - t) for t in range(steps)]

    def edges_of(known):
        return [edge_copies(0, h_old, EDGE - known), edge_copies(1, cell_old, EDGE - 1 - known)]

    def each_layer(act):
        for known in range(layers):

            @pl.when(layer == known)
            def _():
                act(known)

    def place(target, staged, start, stop):
        target[pl.ds(PAD + start, stop - start)] = jnp.swapaxes(staged[:, start:stop], 0, 1)

    def shift_into(center, shifted, start, count):
        above, below = row_shifts(center[pl.ds(start, count)])
        shifted[0, pl.ds(start, count)] = above
        shifted[1, pl.ds(start, count)] = below

    def start_edges(edges):
        edges[0].start()

        @pl.when(jnp.logical_not(first))
        def _():
            edges[1].start()

    def greet():
        awaited = 3 - (layer == layers - 1).astype(jnp.int32) - first.astype(jnp.int32)
        pl.semaphore_wait(barrier, awaited)

        @pl.when(last)
        def _():
            pl.semaphore_signal(late_sem, inc=1, device_id=(layer, right), device_id_type=MESH)

    def send_edges():
        def send(known):
            edges_h, edges_c = edges_of(known)
            start_edges(edges_h)
            if known == 0:
                start_edges(edges_u[0])
            start_edges(edges_c)

        each_layer(send)

    def send_edges_late():
        pl.semaphore_wait(late_sem, 1)

        def send(known):
            edges_h, edges_c = edges_of(known)
            edges_h[1].start()
            if known == 0:
                edges_u[0][1].start()
            edges_c[1].start()
            if known == 0:
                edges_u[1][1].start()

        each_layer(send)

    early = jnp.logical_and(base, last)

    @pl.when(early)
    def _():
        greet()

    load_h.wait()
    place(h_old, stage_h, 0, cols)

    @pl.when(early)
    def _():
        start_edges(edges_of(0)[0])

    @pl.when(base)
    def _():
        load_u[0].wait()
        place(uc.at[0], stage_u.at[0], 0, cols)

    @pl.when(early)
    def _():
        start_edges(edges_u[0])

    load_c.wait()
    place(cell_old, stage_c, 0, cols)

    @pl.when(early)
    def _():
        start_edges(edges_of(0)[1])

    @pl.when(jnp.logical_and(base, jnp.logical_not(jnp.logical_or(last, far))))
    def _():
        greet()
        send_edges()

    shift_into(h_old, hs.at[0], PAD, cols)

    @pl.when(base)
    def _():
        shift_into(uc.at[0], us.at[0], PAD, cols)

    def load_second_input():
        load_u[1].wait()
        place(uc.at[1], stage_u.at[1], 0, cols)
        start_edges(edges_u[1])
        shift_into(uc.at[1], us.at[1], PAD, cols)

    pl.when(early)(load_second_input)

    def finish_edges(which):
        def act(known):
            for edges in edges_of(known):
                edges[which].wait_recv()
            width = EDGE - known
            start = (PAD - width, PAD + cols)[which]
            shift_into(h_old, hs.at[0], start, width)
            if known == 0:
                edges_u[0][which].wait_recv()
                shift_into(uc.at[0], us.at[0], start, width)

        each_layer(act)

    def finish_second_input(which):
        @pl.when(base)
        def _():
            edges_u[1][which].wait_recv()
            shift_into(uc.at[1], us.at[1], (PAD - EDGE + 1, PAD + cols)[which], EDGE - 1)

    def on_side(chunk, act):
        left_now = flipped if chunk == "side" else jnp.logical_not(flipped)

        @pl.when(left_now)
        def _():
            act(0)

        @pl.when(jnp.logical_not(left_now))
        def _():
            act(1)

    def spans(depth, chunk):
        if chunk == "mid":
            return (PAD + 8 + depth,), 16 - 2 * depth
        if chunk == "near":
            return (PAD + 1 + depth, PAD + 24 - depth), 7
        to_left, to_right = PAD - 4 + depth, PAD + 31 - depth
        left_now = flipped if chunk == "side" else jnp.logical_not(flipped)
        return (jnp.where(left_now, to_left, to_right),), 5

    def to_next(t, chunk, pieces):
        return [
            pltpu.make_async_remote_copy(
                src_ref=h_new.at[t, pl.ds(start, count)],
                dst_ref=uc.at[t, pl.ds(start, count)],
                send_sem=next_send.at[t, CHUNKS.index(chunk), i],
                recv_sem=next_recv.at[t, CHUNKS.index(chunk), i],
                device_id=(layer + 1, sector),
                device_id_type=MESH,
            )
            for i, (start, count) in enumerate(pieces)
        ]

    def each_piece(t, chunk, source, act):
        def each(known):
            starts, count = spans(known + t, chunk)
            pieces = tuple((start, count) for start in starts)
            for copy, piece in zip(to_next(t, chunk, pieces), pieces):
                act(copy, piece)

        if chunk == "mid":
            for known in range(layers - 1):
                pl.when(source == known)(lambda known=known: each(known))
        else:
            pl.when(jnp.logical_and(source >= 0, source < layers - 1))(lambda: each(source))

    def receive(t, chunk):
        def act(copy, piece):
            copy.wait_recv()
            shift_into(uc.at[t], us.at[t], *piece)

        each_piece(t, chunk, layer - 1, act)

    def windows(center, shifted, starts, count):
        pick = (lambda s: shifted[0, s], lambda s: center[s], lambda s: shifted[1, s])
        return [
            jnp.concatenate([pick[a](pl.ds(start + b - 1, count)).reshape(-1, chans) for start in starts], axis=0)
            for a in range(3)
            for b in range(3)
        ]

    def product(parts, filters):
        return jnp.dot(
            jnp.concatenate(parts, axis=1), filters.reshape(-1, 4 * chans), preferred_element_type=jnp.float32
        )

    def update(t, starts, count, sums):
        memory = jnp.concatenate([cell_at[t][pl.ds(start, count)].reshape(-1, chans) for start in starts], axis=0)
        hidden, memory = gate_update(sums, memory)
        hidden = hidden.astype(jnp.bfloat16).reshape(len(starts), count, rows, chans)
        memory = memory.reshape(len(starts), count, rows, chans)
        for i, start in enumerate(starts):
            h_new[t, pl.ds(start, count)] = hidden[i]
            cell_at[t + 1][pl.ds(start, count)] = memory[i]
        if t + 1 < steps:
            for i, start in enumerate(starts):
                above, below = row_shifts(hidden[i])
                hs[t + 1, 0, pl.ds(start, count)] = above
                hs[t + 1, 1, pl.ds(start, count)] = below

    partial = {"mid": partial_mid, "near": partial_near}

    def by_layer(chunk, act):
        if chunk == "mid":
            for known in range(layers):
                pl.when(layer == known)(lambda known=known: act(known > 0, known))
        else:
            pl.when(base)(lambda: act(False, 0))
            pl.when(upper)(lambda: act(True, layer))

    def prepare(t, chunk):
        def act(above_first, own):
            if above_first:
                starts, count = spans(own + t, chunk)
                sums = product(windows(h_at[t], hs.at[t], starts, count), w[:, chans:]) + bias[...]
                partial[chunk][pl.ds(0, sums.shape[0])] = sums

        by_layer(chunk, act)

    def compute(t, chunk):
        def whole(own):
            starts, count = spans(own + t, chunk)
            pairs = zip(windows(uc.at[t], us.at[t], starts, count), windows(h_at[t], hs.at[t], starts, count))
            update(t, starts, count, product([part for pair in pairs for part in pair], w[...]) + bias[...])

        def act(above_first, own):
            if above_first:
                starts, count = spans(own + t, chunk)
                sums = product(windows(uc.at[t], us.at[t], starts, count), w[:, :chans])
                update(t, starts, count, sums + partial[chunk][pl.ds(0, sums.shape[0])])
            else:
                whole(own)

        if chunk in partial:
            by_layer(chunk, act)
        else:
            whole(layer)

    def write_columns(t, start, stop):
        h_out[t, :, start:stop] = jnp.swapaxes(h_new[t, PAD + start : PAD + stop], 0, 1)
        if t == steps - 1:
            cell_out[:, start:stop] = jnp.swapaxes(cell_new[PAD + start : PAD + stop], 0, 1)

    for copy in load_w:
        copy.wait()
    load_b.wait()

    @pl.when(upper)
    def _():
        prepare(0, "mid")
        prepare(0, "near")
        greet()
        send_edges()

    for t, chunk in ORDER:
        if (t, chunk) == (0, "side"):
            pl.when(jnp.logical_and(first, base))(send_edges_late)
        if (t, chunk) == (0, "other"):

            @pl.when(upper)
            def _():
                for s in range(steps):
                    write_columns(s, 8, cols - 8)

        if chunk in ("side", "other"):
            on_side(chunk, finish_second_input if t else finish_edges)
        receive(t, chunk)
        compute(t, chunk)
        if (t, chunk) == (0, "mid"):

            @pl.when(jnp.logical_and(base, far))
            def _():
                greet()
                send_edges()

        each_piece(t, chunk, layer, lambda copy, piece: copy.start())
        if (t, chunk) == (0, "mid"):
            pl.when(jnp.logical_and(base, jnp.logical_not(last)))(load_second_input)
            prepare(1, "mid")
        if (t, chunk) == (0, "near"):

            @pl.when(upper)
            def _():
                pl.when(first)(send_edges_late)
                prepare(1, "near")

    for t in range(steps):
        write_columns(t, 0, 8)
        write_columns(t, cols - 8, cols)

    @pl.when(base)
    def _():
        for t in range(steps):
            write_columns(t, 8, cols - 8)

    def sent(known):
        for edges in edges_of(known) + (edges_u if known == 0 else []):
            for copy in edges:
                copy.wait_send()

    each_layer(sent)
    for t, chunk in ORDER:
        each_piece(t, chunk, layer, lambda copy, piece: copy.wait_send())


def finish(h_ref, cell_ref, hidden_out, cell_out, sems):
    copies = [pltpu.make_async_copy(h_ref.at[t], hidden_out.at[0, t], sems.at[t]) for t in range(h_ref.shape[0])]
    copies.append(pltpu.make_async_copy(cell_ref, cell_out.at[0], sems.at[h_ref.shape[0]]))
    for copy in copies:
        copy.start()
    for copy in copies:
        copy.wait()


def solution(mesh):
    layers, sectors = mesh.shape["layer"], mesh.shape["lon"]

    def local(frames, weights, biases, hidden_init, cell_init):
        steps, rows, cols, chans = frames.shape
        bf16, f32 = jnp.bfloat16, jnp.float32
        in_hbm = pl.BlockSpec(memory_space=pltpu.HBM)
        in_vmem = pl.BlockSpec(memory_space=pltpu.VMEM)
        operands = [
            pltpu.with_memory_space_constraint(x, pltpu.HBM)
            for x in (frames, weights, biases, hidden_init, cell_init)
        ]
        hidden, memory = pl.pallas_call(
            lambda *refs: kernel(layers, sectors, *refs),
            out_shape=[
                pltpu.VMEM((steps, rows, cols, chans), bf16),
                pltpu.VMEM((rows, cols, chans), f32),
            ],
            in_specs=[in_hbm] * 5,
            out_specs=[in_vmem] * 2,
            scratch_shapes=[
                pltpu.VMEM((9, 2 * chans, 4 * chans), bf16),
                pltpu.VMEM((1, 4 * chans), f32),
                pltpu.VMEM((rows, cols, chans), bf16),
                pltpu.VMEM((rows, cols, chans), f32),
                pltpu.VMEM((steps, rows, cols, chans), bf16),
                pltpu.VMEM((WIDTH, rows, chans), bf16),
                pltpu.VMEM((steps, WIDTH, rows, chans), bf16),
                pltpu.VMEM((steps, 2, WIDTH, rows, chans), bf16),
                pltpu.VMEM((steps, WIDTH, rows, chans), bf16),
                pltpu.VMEM((steps, 2, WIDTH, rows, chans), bf16),
                pltpu.VMEM((WIDTH, rows, chans), f32),
                pltpu.VMEM((WIDTH, rows, chans), f32),
                pltpu.VMEM((WIDTH, rows, chans), f32),
                pltpu.VMEM((16 * rows, 4 * chans), f32),
                pltpu.VMEM((14 * rows, 4 * chans), f32),
                pltpu.SemaphoreType.DMA((5,)),
                pltpu.SemaphoreType.DMA((9,)),
                pltpu.SemaphoreType.DMA((8,)),
                pltpu.SemaphoreType.DMA((8,)),
                pltpu.SemaphoreType.DMA((steps, 4, 2)),
                pltpu.SemaphoreType.DMA((steps, 4, 2)),
                pltpu.SemaphoreType.REGULAR,
            ],
            compiler_params=pltpu.CompilerParams(
                collective_id=0, has_side_effects=True, vmem_limit_bytes=40 * 1024 * 1024
            ),
            name="conv_lstm",
        )(*operands)
        hidden = pltpu.with_memory_space_constraint(hidden, pltpu.VMEM)
        memory = pltpu.with_memory_space_constraint(memory, pltpu.VMEM)
        return pl.pallas_call(
            finish,
            out_shape=[
                jax.ShapeDtypeStruct((1, steps, rows, cols, chans), bf16),
                jax.ShapeDtypeStruct((1, rows, cols, chans), f32),
            ],
            in_specs=[in_vmem] * 2,
            out_specs=[in_hbm] * 2,
            scratch_shapes=[pltpu.SemaphoreType.DMA((steps + 1,))],
            compiler_params=pltpu.CompilerParams(vmem_limit_bytes=16 * 1024 * 1024),
            name="write_out",
        )(hidden, memory)

    in_specs = (
        P(None, None, "lon", None),
        P("layer", None, None, None),
        P("layer", None),
        P("layer", None, "lon", None),
        P("layer", None, "lon", None),
    )
    out_specs = (P("layer", None, None, "lon", None), P("layer", None, "lon", None))
    return jax.shard_map(local, mesh=mesh, in_specs=in_specs, out_specs=out_specs, check_vma=False)
```

```python
import jax
import jax.numpy as jnp
from jax import lax
from jax.experimental import pallas as pl
from jax.experimental.pallas import tpu as pltpu
from jax.sharding import PartitionSpec as P

MESH = pl.DeviceIdType.MESH
PAD = 8
WIDTH = 48
EDGE = 5
BLOCKS = (
    ((0, "mid"),), ((0, "near"),), ((1, "mid"),), ((1, "near"),), ((0, "side"),), ((1, "side"),), ((0, "other"),), ((1, "other"),),
)
CHUNKS = ("mid", "near", "side", "other")


def row_shifts(columns):
    blank = jnp.zeros((columns.shape[0], 1, columns.shape[2]), columns.dtype)
    above = jnp.concatenate([blank, columns[:, :-1]], axis=1)
    below = jnp.concatenate([columns[:, 1:], blank], axis=1)
    return above, below


def gate_update(gate_sums, memory):
    chans = memory.shape[-1]
    ingate = 0.5 * jnp.tanh(0.5 * gate_sums[:, :chans]) + 0.5
    forget = 0.5 * jnp.tanh(0.5 * gate_sums[:, chans : 2 * chans]) + 0.5
    candidate = jnp.tanh(gate_sums[:, 2 * chans : 3 * chans])
    outgate = 0.5 * jnp.tanh(0.5 * gate_sums[:, 3 * chans :]) + 0.5
    new_memory = forget * memory + ingate * candidate
    return outgate * jnp.tanh(new_memory), new_memory


def kernel(layers, sectors, *refs):
    for layer in range(layers):
        pl.when(lax.axis_index("layer") == layer)(lambda layer=layer: layer_program(layer, layers, sectors, *refs))


def layer_program(
    layer, layers, sectors,
    frames, weights, biases, hidden_init, cell_init, h_out, cell_out,
    w, bias, stage_h, stage_c, stage_u, h_old, h_new, hs, uc, us, cell_old, cell_edge, cell_mid, cell_new,
    partial_mid, partial_near, load_sem, w_sem, edge_send, edge_recv, next_send, next_recv, late_sem,
):
    sector = lax.axis_index("lon")
    right, left = lax.rem(sector + 1, sectors), lax.rem(sector + sectors - 1, sectors)
    steps, rows, cols, chans = stage_u.shape
    base, top = layer == 0, layer == layers - 1
    first, last = sector == 0, sector == sectors - 1
    far_or_last = jnp.logical_or(jnp.logical_or(sector == sectors // 2 - 1, sector == sectors // 2), last)
    flipped = lax.rem(sector, 4) == 3
    h_at = [h_old] + [h_new.at[t] for t in range(steps)]
    cell_at = [cell_old, cell_mid, cell_new]
    partial = {"mid": partial_mid, "near": partial_near}

    load_h = pltpu.make_async_copy(hidden_init.at[0], stage_h, load_sem.at[0])
    load_c = pltpu.make_async_copy(cell_init.at[0], stage_c, load_sem.at[1])
    load_u = [pltpu.make_async_copy(frames.at[t], stage_u.at[t], load_sem.at[2 + t]) for t in range(steps)]
    load_b = pltpu.make_async_copy(biases, bias, load_sem.at[4])
    load_w = [pltpu.make_async_copy(weights.at[0, i], w.at[i], w_sem.at[i]) for i in range(9)]

    barrier = pltpu.get_barrier_semaphore()
    load_h.start()
    if base:
        load_u[0].start()
    pl.semaphore_signal(barrier, inc=1, device_id=(layer, left), device_id_type=MESH)

    @pl.when(jnp.logical_not(last))
    def _():
        pl.semaphore_signal(barrier, inc=1, device_id=(layer, right), device_id_type=MESH)

    if not base:
        pl.semaphore_signal(barrier, inc=1, device_id=(layer - 1, sector), device_id_type=MESH)
    load_c.start()
    for copy in load_w:
        copy.start()
    load_b.start()
    if base:
        load_u[1].start()

    def edge_copies(index, buffer, width):
        return [
            pltpu.make_async_remote_copy(
                src_ref=buffer.at[pl.ds(source, width)],
                dst_ref=buffer.at[pl.ds(target, width)],
                send_sem=edge_send.at[2 * index + which],
                recv_sem=edge_recv.at[2 * index + which],
                device_id=(layer, side),
                device_id_type=MESH,
            )
            for side, source, target, which in (
                (right, PAD + cols - width, PAD - width, 0),
                (left, PAD, PAD + cols, 1),
            )
        ]

    width = EDGE - layer
    edges_h = edge_copies(0, h_old, width)
    edges_c = edge_copies(1, cell_edge, width - 1)
    edges_u = [edge_copies(2 + t, uc.at[t], width - t) for t in range(steps)] if base else []
    soon = [edges_h] + edges_u[:1] + [edges_c]

    def place(target, staged, start, stop):
        target[pl.ds(PAD + start, stop - start)] = jnp.swapaxes(staged[:, start:stop], 0, 1)

    def shift_into(center, shifted, start, count):
        above, below = row_shifts(center[pl.ds(start, count)])
        shifted[0, pl.ds(start, count)] = above
        shifted[1, pl.ds(start, count)] = below

    def start_edges(groups):
        for edges in groups:
            edges[0].start()

        @pl.when(jnp.logical_not(first))
        def _():
            for edges in groups:
                edges[1].start()

    def start_edges_late():
        pl.semaphore_wait(late_sem, 1)
        for edges in soon + edges_u[1:]:
            edges[1].start()

    def greet():
        pl.semaphore_wait(barrier, (2 if top else 3) - first.astype(jnp.int32))

    @pl.when(last)
    def _():
        greet()
        pl.semaphore_signal(late_sem, inc=1, device_id=(layer, right), device_id_type=MESH)

    load_h.wait()
    place(h_old, stage_h, 0, cols)
    if base:
        pl.when(last)(lambda: start_edges([edges_h]))
        load_u[0].wait()
        place(uc.at[0], stage_u.at[0], 0, cols)
        pl.when(last)(lambda: start_edges([edges_u[0]]))
    shift_into(h_old, hs.at[0], PAD, cols)
    if base:
        shift_into(uc.at[0], us.at[0], PAD, cols)
    load_c.wait()
    place(cell_old, stage_c, 0, cols)
    for start in (PAD, PAD + cols - EDGE + 1):
        cell_edge[pl.ds(start, EDGE - 1)] = cell_old[pl.ds(start, EDGE - 1)].astype(jnp.bfloat16)
    if base:
        pl.when(last)(lambda: start_edges([edges_c]))

    def load_second_input():
        load_u[1].wait()
        place(uc.at[1], stage_u.at[1], 0, cols)
        start_edges([edges_u[1]])
        shift_into(uc.at[1], us.at[1], PAD, cols)

    def finish_edges(which):
        edges_h[which].wait_recv()
        edges_c[which].wait_recv()
        start = (PAD - width, PAD + cols)[which]
        shift_into(h_old, hs.at[0], start, width)
        edge = pl.ds((PAD - width + 1, PAD + cols)[which], width - 1)
        cell_old[edge] = cell_edge[edge].astype(jnp.float32)
        if base:
            edges_u[0][which].wait_recv()
            shift_into(uc.at[0], us.at[0], start, width)

    def finish_second_input(which):
        edges_u[1][which].wait_recv()
        shift_into(uc.at[1], us.at[1], (PAD - EDGE + 1, PAD + cols)[which], EDGE - 1)

    def is_left(chunk):
        return flipped if chunk == "side" else jnp.logical_not(flipped)

    def on_side(chunk, act):
        pl.when(is_left(chunk))(lambda: act(0))
        pl.when(jnp.logical_not(is_left(chunk)))(lambda: act(1))

    def spans(depth, chunk):
        if chunk == "mid":
            return (PAD + 8 + depth,), 16 - 2 * depth
        if chunk == "near":
            return (PAD + 1 + depth, PAD + 24 - depth), 7
        return (jnp.where(is_left(chunk), PAD - 4 + depth, PAD + 31 - depth),), 5

    def to_next(t, chunk, source):
        starts, count = spans(source + t, chunk)
        return [
            (
                pltpu.make_async_remote_copy(
                    src_ref=h_new.at[t, pl.ds(start, count)],
                    dst_ref=uc.at[t, pl.ds(start, count)],
                    send_sem=next_send.at[t, CHUNKS.index(chunk), i],
                    recv_sem=next_recv.at[t, CHUNKS.index(chunk), i],
                    device_id=(source + 1, sector),
                    device_id_type=MESH,
                ),
                start,
                count,
            )
            for i, start in enumerate(starts)
        ]

    def windows(center, shifted, starts, count):
        pick = (lambda s: shifted[0, s], lambda s: center[s], lambda s: shifted[1, s])
        return [
            jnp.concatenate([pick[a](pl.ds(start + b - 1, count)).reshape(-1, chans) for start in starts], axis=0)
            for a in range(3)
            for b in range(3)
        ]

    def product(parts, filters):
        return jnp.dot(
            jnp.concatenate(parts, axis=1), filters.reshape(-1, 4 * chans), preferred_element_type=jnp.float32
        )

    def prepare(t, chunk):
        starts, count = spans(layer + t, chunk)
        sums = product(windows(h_at[t], hs.at[t], starts, count), w[:, chans:]) + bias[...]
        partial[chunk][pl.ds(0, sums.shape[0])] = sums

    def compute(t, chunk):
        starts, count = spans(layer + t, chunk)
        inputs = windows(uc.at[t], us.at[t], starts, count)
        if chunk in partial and not base:
            sums = product(inputs, w[:, :chans])
            sums = sums + partial[chunk][pl.ds(0, sums.shape[0])]
        else:
            pairs = zip(inputs, windows(h_at[t], hs.at[t], starts, count))
            sums = product([part for pair in pairs for part in pair], w[...]) + bias[...]
        memory = jnp.concatenate([cell_at[t][pl.ds(start, count)].reshape(-1, chans) for start in starts], axis=0)
        hidden, memory = gate_update(sums, memory)
        hidden = hidden.astype(jnp.bfloat16).reshape(len(starts), count, rows, chans)
        memory = memory.reshape(len(starts), count, rows, chans)
        for i, start in enumerate(starts):
            h_new[t, pl.ds(start, count)] = hidden[i]
            cell_at[t + 1][pl.ds(start, count)] = memory[i]
        if t + 1 < steps:
            for i, start in enumerate(starts):
                above, below = row_shifts(hidden[i])
                hs[t + 1, 0, pl.ds(start, count)] = above
                hs[t + 1, 1, pl.ds(start, count)] = below

    def write_columns(t, start, stop):
        h_out[t, :, start:stop] = jnp.swapaxes(h_new[t, PAD + start : PAD + stop], 0, 1)
        if t == steps - 1:
            cell_out[:, start:stop] = jnp.swapaxes(cell_new[PAD + start : PAD + stop], 0, 1)

    for copy in load_w:
        copy.wait()
    load_b.wait()
    if not base:
        prepare(0, "mid")
        prepare(0, "near")
        pl.when(jnp.logical_not(last))(greet)
        if layer == 1:
            pl.when(far_or_last)(lambda: start_edges(soon))
        else:
            start_edges(soon)

    for block in BLOCKS:
        if (0, "side") in block:
            if base:
                pl.when(first)(start_edges_late)
            on_side("side", finish_edges)
        if (0, "other") in block:
            on_side("other", finish_edges)
        if (1, "side") in block and base:
            on_side("side", finish_second_input)
        if (1, "other") in block:
            if base:
                on_side("other", finish_second_input)
            else:
                for t in range(steps):
                    write_columns(t, 8, cols - 8)
        if not base:
            arrivals = [(t, *item) for t, chunk in block for item in to_next(t, chunk, layer - 1)]
            for _, copy, _, _ in arrivals:
                copy.wait_recv()
            for t, _, start, count in arrivals:
                shift_into(uc.at[t], us.at[t], start, count)
        for t, chunk in block:
            compute(t, chunk)
        if base and block == BLOCKS[0]:

            @pl.when(jnp.logical_not(last))
            def _():
                greet()
                start_edges(soon)

        if not top:
            for t, chunk in block:
                for copy, _, _ in to_next(t, chunk, layer):
                    copy.start()
        if block == BLOCKS[0]:
            if base:
                load_second_input()
            else:
                if layer == 1:
                    pl.when(jnp.logical_not(far_or_last))(lambda: start_edges(soon))
                prepare(1, "mid")
        if block == BLOCKS[1] and not base:
            prepare(1, "near")
        if block == BLOCKS[2] and not base:
            pl.when(first)(start_edges_late)

    for t in range(steps):
        write_columns(t, 0, 8)
        write_columns(t, cols - 8, cols)
    if base:
        for t in range(steps):
            write_columns(t, 8, cols - 8)

    for edges in soon + edges_u[1:]:
        for copy in edges:
            copy.wait_send()
    if not top:
        for block in BLOCKS:
            for t, chunk in block:
                for copy, _, _ in to_next(t, chunk, layer):
                    copy.wait_send()


def finish(h_ref, cell_ref, hidden_out, cell_out, sems):
    steps, rows = h_ref.shape[:2]
    half = rows // 2
    copies = []
    for start in (0, half):
        part = pl.ds(start, half)
        pairs = [(h_ref.at[t, part], hidden_out.at[0, t, part]) for t in range(steps)]
        for source, target in pairs + [(cell_ref.at[part], cell_out.at[0, part])]:
            copies.append(pltpu.make_async_copy(source, target, sems.at[len(copies)]))
            copies[-1].start()
    for copy in copies:
        copy.wait()


def solution(mesh):
    layers, sectors = mesh.shape["layer"], mesh.shape["lon"]

    def local(frames, weights, biases, hidden_init, cell_init):
        steps, rows, cols, chans = frames.shape
        bf16, f32 = jnp.bfloat16, jnp.float32
        in_hbm = pl.BlockSpec(memory_space=pltpu.HBM)
        in_vmem = pl.BlockSpec(memory_space=pltpu.VMEM)
        operands = [
            pltpu.with_memory_space_constraint(x, pltpu.HBM)
            for x in (frames, weights, biases, hidden_init, cell_init)
        ]
        hidden, memory = pl.pallas_call(
            lambda *refs: kernel(layers, sectors, *refs),
            out_shape=[
                pltpu.VMEM((steps, rows, cols, chans), bf16),
                pltpu.VMEM((rows, cols, chans), f32),
            ],
            in_specs=[in_hbm] * 5,
            out_specs=[in_vmem] * 2,
            scratch_shapes=[
                pltpu.VMEM((9, 2 * chans, 4 * chans), bf16),
                pltpu.VMEM((1, 4 * chans), f32),
                pltpu.VMEM((rows, cols, chans), bf16),
                pltpu.VMEM((rows, cols, chans), f32),
                pltpu.VMEM((steps, rows, cols, chans), bf16),
                pltpu.VMEM((WIDTH, rows, chans), bf16),
                pltpu.VMEM((steps, WIDTH, rows, chans), bf16),
                pltpu.VMEM((steps, 2, WIDTH, rows, chans), bf16),
                pltpu.VMEM((steps, WIDTH, rows, chans), bf16),
                pltpu.VMEM((steps, 2, WIDTH, rows, chans), bf16),
                pltpu.VMEM((WIDTH, rows, chans), f32),
                pltpu.VMEM((WIDTH, rows, chans), bf16),
                pltpu.VMEM((WIDTH, rows, chans), f32),
                pltpu.VMEM((WIDTH, rows, chans), f32),
                pltpu.VMEM((16 * rows, 4 * chans), f32),
                pltpu.VMEM((14 * rows, 4 * chans), f32),
                pltpu.SemaphoreType.DMA((5,)),
                pltpu.SemaphoreType.DMA((9,)),
                pltpu.SemaphoreType.DMA((8,)),
                pltpu.SemaphoreType.DMA((8,)),
                pltpu.SemaphoreType.DMA((steps, 4, 2)),
                pltpu.SemaphoreType.DMA((steps, 4, 2)),
                pltpu.SemaphoreType.REGULAR,
            ],
            compiler_params=pltpu.CompilerParams(
                collective_id=0, has_side_effects=True, vmem_limit_bytes=40 * 1024 * 1024
            ),
            name="conv_lstm",
        )(*operands)
        hidden = pltpu.with_memory_space_constraint(hidden, pltpu.VMEM)
        memory = pltpu.with_memory_space_constraint(memory, pltpu.VMEM)
        return pl.pallas_call(
            finish,
            out_shape=[
                jax.ShapeDtypeStruct((1, steps, rows, cols, chans), bf16),
                jax.ShapeDtypeStruct((1, rows, cols, chans), f32),
            ],
            in_specs=[in_vmem] * 2,
            out_specs=[in_hbm] * 2,
            scratch_shapes=[pltpu.SemaphoreType.DMA((2 * steps + 2,))],
            compiler_params=pltpu.CompilerParams(vmem_limit_bytes=16 * 1024 * 1024),
            name="write_out",
        )(hidden, memory)

    in_specs = (
        P(None, None, "lon", None),
        P("layer", None, None, None),
        P("layer", None),
        P("layer", None, "lon", None),
        P("layer", None, "lon", None),
    )
    out_specs = (P("layer", None, None, "lon", None), P("layer", None, "lon", None))
    return jax.shard_map(local, mesh=mesh, in_specs=in_specs, out_specs=out_specs, check_vma=False)
```

```python
import jax
import jax.numpy as jnp
from jax import lax
from jax.experimental import pallas as pl
from jax.experimental.pallas import tpu as pltpu
from jax.sharding import PartitionSpec as P

MESH = pl.DeviceIdType.MESH
PAD = 8
WIDTH = 48
EDGE = 5
BLOCKS = (
    ((0, "mid"),), ((0, "near"),), ((1, "mid"),), ((1, "near"),), ((0, "side"),), ((1, "side"),), ((0, "other"),), ((1, "other"),),
)
CHUNKS = ("mid", "near", "side", "other")


def row_shifts(columns):
    blank = jnp.zeros((columns.shape[0], 1, columns.shape[2]), columns.dtype)
    above = jnp.concatenate([blank, columns[:, :-1]], axis=1)
    below = jnp.concatenate([columns[:, 1:], blank], axis=1)
    return above, below


def gate_update(gate_sums, memory):
    chans = memory.shape[-1]
    ingate = 0.5 * jnp.tanh(0.5 * gate_sums[:, :chans]) + 0.5
    forget = 0.5 * jnp.tanh(0.5 * gate_sums[:, chans : 2 * chans]) + 0.5
    candidate = jnp.tanh(gate_sums[:, 2 * chans : 3 * chans])
    outgate = 0.5 * jnp.tanh(0.5 * gate_sums[:, 3 * chans :]) + 0.5
    new_memory = forget * memory + ingate * candidate
    return outgate * jnp.tanh(new_memory), new_memory


def kernel(layers, sectors, *refs):
    for layer in range(layers):
        pl.when(lax.axis_index("layer") == layer)(lambda layer=layer: layer_program(layer, layers, sectors, *refs))


def layer_program(
    layer, layers, sectors,
    frames, weights, biases, hidden_init, cell_init, h_out, cell_out,
    w, bias, stage_h, stage_c, stage_u, u_far, h_old, h_new, hs, uc, us, cell_old, cell_edge, cell_mid, cell_new,
    partial_mid, partial_near, load_sem, edge_send, edge_recv, next_send, next_recv, late_sem,
):
    sector = lax.axis_index("lon")
    right, left = lax.rem(sector + 1, sectors), lax.rem(sector + sectors - 1, sectors)
    steps, rows, cols, chans = stage_u.shape
    base, top = layer == 0, layer == layers - 1
    first, last = sector == 0, sector == sectors - 1
    far_right = jnp.logical_or(sector == sectors // 2 - 1, last)
    far_left = jnp.logical_or(sector == sectors // 2, first)
    far = jnp.logical_or(far_right, far_left)
    far_or_last = jnp.logical_and(far, jnp.logical_not(first))
    flipped = lax.rem(sector, 4) == 3
    h_at = [h_old] + [h_new.at[t] for t in range(steps)]
    cell_at = [cell_old, cell_mid, cell_new]
    partial = {"mid": partial_mid, "near": partial_near}

    load_h = pltpu.make_async_copy(hidden_init.at[0], stage_h, load_sem.at[0])
    load_c = pltpu.make_async_copy(cell_init.at[0], stage_c, load_sem.at[1])
    load_u = [pltpu.make_async_copy(frames.at[t], stage_u.at[t], load_sem.at[2 + t]) for t in range(steps)]
    load_b = pltpu.make_async_copy(biases, bias, load_sem.at[4])
    load_w = [pltpu.make_async_copy(weights.at[0, i], w.at[i], load_sem.at[5]) for i in range(9)]

    barrier = pltpu.get_barrier_semaphore()
    load_h.start()
    if base:
        load_u[0].start()
    pl.semaphore_signal(barrier, inc=1, device_id=(layer, left), device_id_type=MESH)

    @pl.when(jnp.logical_not(last))
    def _():
        pl.semaphore_signal(barrier, inc=1, device_id=(layer, right), device_id_type=MESH)

    if not base:
        pl.semaphore_signal(barrier, inc=1, device_id=(layer - 1, sector), device_id_type=MESH)
    else:
        @pl.when(far)
        def _():
            pl.semaphore_signal(barrier, inc=1, device_id=(layers - 1, sectors - 1 - sector), device_id_type=MESH)

    if top:

        @pl.when(far)
        def _():
            for copy in load_u:
                copy.start()

    load_c.start()
    for copy in load_w:
        copy.start()
    load_b.start()
    if base:
        load_u[1].start()

    def wait_columns(sem, count):
        pair = hs.at[0, :, pl.ds(0, count // 2)] if count % 2 == 0 else hs.at[0, 0, pl.ds(0, count)]
        pltpu.make_async_copy(pair, pair, sem).wait()

    def edge_copies(index, buffer, width):
        return [
            pltpu.make_async_remote_copy(
                src_ref=buffer.at[pl.ds(source, width)],
                dst_ref=buffer.at[pl.ds(target, width)],
                send_sem=edge_send,
                recv_sem=edge_recv.at[2 * index + which],
                device_id=(layer, side),
                device_id_type=MESH,
            )
            for side, source, target, which in (
                (right, PAD + cols - width, PAD - width, 0),
                (left, PAD, PAD + cols, 1),
            )
        ]

    width = EDGE - layer
    edges_h = edge_copies(0, h_old, width)
    edges_c = edge_copies(0, cell_edge, width - 1)
    edges_u = [edge_copies(t, uc.at[t], width - t) for t in range(steps)] if base else []
    soon = [edges_h, edges_c]

    def place(target, staged, start, stop):
        target[pl.ds(PAD + start, stop - start)] = jnp.swapaxes(staged[:, start:stop], 0, 1)

    def shift_into(center, shifted, start, count):
        above, below = row_shifts(center[pl.ds(start, count)])
        shifted[0, pl.ds(start, count)] = above
        shifted[1, pl.ds(start, count)] = below

    def start_edges(groups):
        for edges in groups:
            edges[0].start()

        @pl.when(jnp.logical_not(first))
        def _():
            for edges in groups:
                edges[1].start()

    def start_inputs(t):
        pl.when(jnp.logical_not(far_right))(edges_u[t][0].start)
        pl.when(jnp.logical_not(far_left))(edges_u[t][1].start)

    def start_edges_late():
        pl.semaphore_wait(late_sem, 1)
        for edges in soon:
            edges[1].start()

    def start_far_inputs():
        for copy in load_u:
            copy.wait()
        for which, chosen, source in ((0, far_right, cols - 8), (1, far_left, 0)):

            @pl.when(chosen)
            def _():
                for t in range(steps):
                    u_far[t] = jnp.swapaxes(stage_u[t, :, source : source + 8], 0, 1)
                for t in range(steps):
                    count = EDGE - t
                    pltpu.make_async_remote_copy(
                        src_ref=u_far.at[t, pl.ds((8 - count, 0)[which], count)],
                        dst_ref=uc.at[t, pl.ds((PAD - count, PAD + cols)[which], count)],
                        send_sem=edge_send,
                        recv_sem=edge_recv.at[2 * t + which],
                        device_id=(0, sectors - 1 - sector),
                        device_id_type=MESH,
                    ).start()

    def greet():
        awaited = 3 - first.astype(jnp.int32)
        if top:
            awaited = awaited - 1 + far.astype(jnp.int32)
        pl.semaphore_wait(barrier, awaited)

    @pl.when(last)
    def _():
        greet()
        pl.semaphore_signal(late_sem, inc=1, device_id=(layer, right), device_id_type=MESH)
        if top:
            start_far_inputs()

    load_h.wait()
    place(h_old, stage_h, 0, cols)
    if base:
        pl.when(last)(lambda: start_edges([edges_h]))
        load_u[0].wait()
        place(uc.at[0], stage_u.at[0], 0, cols)
        pl.when(last)(lambda: start_inputs(0))
    shift_into(h_old, hs.at[0], PAD, cols)
    if base:
        shift_into(uc.at[0], us.at[0], PAD, cols)
    load_c.wait()
    place(cell_old, stage_c, 0, cols)
    for start in (PAD, PAD + cols - EDGE + 1):
        cell_edge[pl.ds(start, EDGE - 1)] = cell_old[pl.ds(start, EDGE - 1)].astype(jnp.bfloat16)
    if base:
        pl.when(last)(lambda: start_edges([edges_c]))

    def finish_edges(which):
        wait_columns(edge_recv.at[which], 3 * width - 1 if base else 2 * width - 1)
        start = (PAD - width, PAD + cols)[which]
        shift_into(h_old, hs.at[0], start, width)
        edge = pl.ds((PAD - width + 1, PAD + cols)[which], width - 1)
        cell_old[edge] = cell_edge[edge].astype(jnp.float32)
        if base:
            shift_into(uc.at[0], us.at[0], start, width)

    def finish_second_input(which):
        wait_columns(edge_recv.at[2 + which], width - 1)
        shift_into(uc.at[1], us.at[1], (PAD - EDGE + 1, PAD + cols)[which], EDGE - 1)

    def is_left(chunk):
        return flipped if chunk == "side" else jnp.logical_not(flipped)

    def on_side(chunk, act):
        pl.when(is_left(chunk))(lambda: act(0))
        pl.when(jnp.logical_not(is_left(chunk)))(lambda: act(1))

    def spans(depth, chunk):
        if chunk == "mid":
            return (PAD + 8 + depth,), 16 - 2 * depth
        if chunk == "near":
            return (PAD + 1 + depth, PAD + 24 - depth), 7
        return (jnp.where(is_left(chunk), PAD - 4 + depth, PAD + 31 - depth),), 5

    def to_next(t, chunk, source):
        starts, count = spans(source + t, chunk)
        return [
            (
                pltpu.make_async_remote_copy(
                    src_ref=h_new.at[t, pl.ds(start, count)],
                    dst_ref=uc.at[t, pl.ds(start, count)],
                    send_sem=next_send,
                    recv_sem=next_recv.at[t, CHUNKS.index(chunk)],
                    device_id=(source + 1, sector),
                    device_id_type=MESH,
                ),
                start,
                count,
            )
            for start in starts
        ]

    def windows(center, shifted, starts, count):
        pick = (lambda s: shifted[0, s], lambda s: center[s], lambda s: shifted[1, s])
        return [
            jnp.concatenate([pick[a](pl.ds(start + b - 1, count)).reshape(-1, chans) for start in starts], axis=0)
            for a in range(3)
            for b in range(3)
        ]

    def product(parts, filters):
        return jnp.dot(
            jnp.concatenate(parts, axis=1), filters.reshape(-1, 4 * chans), preferred_element_type=jnp.float32
        )

    def prepare(t, chunk):
        starts, count = spans(layer + t, chunk)
        sums = product(windows(h_at[t], hs.at[t], starts, count), w[:, chans:]) + bias[...]
        partial[chunk][pl.ds(0, sums.shape[0])] = sums

    def compute(t, chunk):
        starts, count = spans(layer + t, chunk)
        inputs = windows(uc.at[t], us.at[t], starts, count)
        if chunk in partial and not base:
            sums = product(inputs, w[:, :chans])
            sums = sums + partial[chunk][pl.ds(0, sums.shape[0])]
        else:
            pairs = zip(inputs, windows(h_at[t], hs.at[t], starts, count))
            sums = product([part for pair in pairs for part in pair], w[...]) + bias[...]
        memory = jnp.concatenate([cell_at[t][pl.ds(start, count)].reshape(-1, chans) for start in starts], axis=0)
        hidden, memory = gate_update(sums, memory)
        hidden = hidden.astype(jnp.bfloat16).reshape(len(starts), count, rows, chans)
        memory = memory.reshape(len(starts), count, rows, chans)
        for i, start in enumerate(starts):
            h_new[t, pl.ds(start, count)] = hidden[i]
            cell_at[t + 1][pl.ds(start, count)] = memory[i]
        if t + 1 < steps:
            for i, start in enumerate(starts):
                above, below = row_shifts(hidden[i])
                hs[t + 1, 0, pl.ds(start, count)] = above
                hs[t + 1, 1, pl.ds(start, count)] = below

    def write_columns(t, start, stop):
        h_out[t, :, start:stop] = jnp.swapaxes(h_new[t, PAD + start : PAD + stop], 0, 1)
        if t == steps - 1:
            cell_out[:, start:stop] = jnp.swapaxes(cell_new[PAD + start : PAD + stop], 0, 1)

    pltpu.make_async_copy(weights.at[0], w, load_sem.at[5]).wait()
    load_b.wait()
    if not base:
        prepare(0, "mid")
        prepare(0, "near")
        pl.when(jnp.logical_not(last))(greet)
        if layer == 1:
            pl.when(far_or_last)(lambda: start_edges(soon))
        else:
            start_edges(soon)
        if top:
            pl.when(jnp.logical_and(far, jnp.logical_not(last)))(start_far_inputs)

    for block in BLOCKS:
        if (0, "side") in block:
            if base:
                pl.when(first)(start_edges_late)
            on_side("side", finish_edges)
        if (0, "other") in block:
            on_side("other", finish_edges)
        if (1, "side") in block and base:
            on_side("side", finish_second_input)
        if (1, "other") in block and base:
            on_side("other", finish_second_input)
        if base:
            if block == BLOCKS[1]:
                load_u[1].wait()
        else:
            arrivals = [(t, chunk, *piece) for t, chunk in block for piece in to_next(t, chunk, layer - 1)]
            for t, chunk in block:
                wait_columns(next_recv.at[t, CHUNKS.index(chunk)], sum(a[4] for a in arrivals if a[:2] == (t, chunk)))
            for t, _, _, start, count in arrivals:
                shift_into(uc.at[t], us.at[t], start, count)
        for t, chunk in block:
            compute(t, chunk)
        if base and block == BLOCKS[0]:

            @pl.when(jnp.logical_not(last))
            def _():
                greet()
                start_edges([edges_h])
                start_inputs(0)
                start_edges([edges_c])

        if base and block == BLOCKS[1]:
            place(uc.at[1], stage_u.at[1], 0, cols)
            shift_into(uc.at[1], us.at[1], PAD, cols)
        if not top:
            for t, chunk in block:
                for copy, _, _ in to_next(t, chunk, layer):
                    copy.start()
        if base and block == BLOCKS[1]:
            start_inputs(1)
        if not base:
            if block == BLOCKS[0]:
                if layer == 1:
                    pl.when(jnp.logical_not(far_or_last))(lambda: start_edges(soon))
                prepare(1, "mid")
            if block == BLOCKS[1]:
                prepare(1, "near")
            if block == BLOCKS[2]:
                pl.when(first)(start_edges_late)

    for t in range(steps):
        write_columns(t, 0, cols)

    sent = 2 * (2 * width - 1)
    inputs = 2 * EDGE - 1
    if base:
        pl.when(far)(lambda: wait_columns(edge_send, sent + inputs))
        pl.when(jnp.logical_not(far))(lambda: wait_columns(edge_send, sent + 2 * inputs))
    elif top:
        pl.when(far)(lambda: wait_columns(edge_send, sent + inputs))
        pl.when(jnp.logical_not(far))(lambda: wait_columns(edge_send, sent))
    else:
        wait_columns(edge_send, sent)
    if not top:
        wait_columns(next_send, sum(piece[2] for block in BLOCKS for t, chunk in block for piece in to_next(t, chunk, layer)))


def finish(h_ref, cell_ref, hidden_out, cell_out, sems):
    copies = [
        pltpu.make_async_copy(h_ref, hidden_out.at[0], sems.at[0]),
        pltpu.make_async_copy(cell_ref, cell_out.at[0], sems.at[1]),
    ]
    for copy in copies:
        copy.start()
    for copy in copies:
        copy.wait()


def solution(mesh):
    layers, sectors = mesh.shape["layer"], mesh.shape["lon"]

    def local(frames, weights, biases, hidden_init, cell_init):
        steps, rows, cols, chans = frames.shape
        bf16, f32 = jnp.bfloat16, jnp.float32
        in_hbm = pl.BlockSpec(memory_space=pltpu.HBM)
        in_vmem = pl.BlockSpec(memory_space=pltpu.VMEM)
        operands = [
            pltpu.with_memory_space_constraint(x, pltpu.HBM)
            for x in (frames, weights, biases, hidden_init, cell_init)
        ]
        hidden, memory = pl.pallas_call(
            lambda *refs: kernel(layers, sectors, *refs),
            out_shape=[
                pltpu.VMEM((steps, rows, cols, chans), bf16),
                pltpu.VMEM((rows, cols, chans), f32),
            ],
            in_specs=[in_hbm] * 5,
            out_specs=[in_vmem] * 2,
            scratch_shapes=[
                pltpu.VMEM((9, 2 * chans, 4 * chans), bf16),
                pltpu.VMEM((1, 4 * chans), f32),
                pltpu.VMEM((rows, cols, chans), bf16),
                pltpu.VMEM((rows, cols, chans), f32),
                pltpu.VMEM((steps, rows, cols, chans), bf16),
                pltpu.VMEM((steps, 8, rows, chans), bf16),
                pltpu.VMEM((WIDTH, rows, chans), bf16),
                pltpu.VMEM((steps, WIDTH, rows, chans), bf16),
                pltpu.VMEM((steps, 2, WIDTH, rows, chans), bf16),
                pltpu.VMEM((steps, WIDTH, rows, chans), bf16),
                pltpu.VMEM((steps, 2, WIDTH, rows, chans), bf16),
                pltpu.VMEM((WIDTH, rows, chans), f32),
                pltpu.VMEM((WIDTH, rows, chans), bf16),
                pltpu.VMEM((WIDTH, rows, chans), f32),
                pltpu.VMEM((WIDTH, rows, chans), f32),
                pltpu.VMEM((16 * rows, 4 * chans), f32),
                pltpu.VMEM((14 * rows, 4 * chans), f32),
                pltpu.SemaphoreType.DMA((6,)),
                pltpu.SemaphoreType.DMA,
                pltpu.SemaphoreType.DMA((4,)),
                pltpu.SemaphoreType.DMA,
                pltpu.SemaphoreType.DMA((steps, 4)),
                pltpu.SemaphoreType.REGULAR,
            ],
            compiler_params=pltpu.CompilerParams(
                collective_id=0, has_side_effects=True, vmem_limit_bytes=40 * 1024 * 1024
            ),
            name="conv_lstm",
        )(*operands)
        hidden = pltpu.with_memory_space_constraint(hidden, pltpu.VMEM)
        memory = pltpu.with_memory_space_constraint(memory, pltpu.VMEM)
        return pl.pallas_call(
            finish,
            out_shape=[
                jax.ShapeDtypeStruct((1, steps, rows, cols, chans), bf16),
                jax.ShapeDtypeStruct((1, rows, cols, chans), f32),
            ],
            in_specs=[in_vmem] * 2,
            out_specs=[in_hbm] * 2,
            scratch_shapes=[pltpu.SemaphoreType.DMA((2,))],
            compiler_params=pltpu.CompilerParams(vmem_limit_bytes=16 * 1024 * 1024),
            name="write_out",
        )(hidden, memory)

    in_specs = (
        P(None, None, "lon", None),
        P("layer", None, None, None),
        P("layer", None),
        P("layer", None, "lon", None),
        P("layer", None, "lon", None),
    )
    out_specs = (P("layer", None, None, "lon", None), P("layer", None, "lon", None))
    return jax.shard_map(local, mesh=mesh, in_specs=in_specs, out_specs=out_specs, check_vma=False)
```

```python
import jax
import jax.numpy as jnp
from jax import lax
from jax.experimental import pallas as pl
from jax.experimental.pallas import tpu as pltpu
from jax.sharding import PartitionSpec as P

MESH = pl.DeviceIdType.MESH
PAD = 8
WIDTH = 48
EDGE = 5
ORDER = (
    (0, "mid"), (0, "near"), (0, "rim"), (1, "mid"), (1, "near"), (1, "rim"),
    (0, "side"), (1, "side"), (0, "other"), (1, "other"),
)
CHUNKS = ("mid", "near", "rim", "side", "other")


def row_shifts(columns):
    blank = jnp.zeros((columns.shape[0], 1, columns.shape[2]), columns.dtype)
    above = jnp.concatenate([blank, columns[:, :-1]], axis=1)
    below = jnp.concatenate([columns[:, 1:], blank], axis=1)
    return above, below


def gate_update(gate_sums, memory):
    chans = memory.shape[-1]
    ingate = 0.5 * jnp.tanh(0.5 * gate_sums[:, :chans]) + 0.5
    forget = 0.5 * jnp.tanh(0.5 * gate_sums[:, chans : 2 * chans]) + 0.5
    candidate = jnp.tanh(gate_sums[:, 2 * chans : 3 * chans])
    outgate = 0.5 * jnp.tanh(0.5 * gate_sums[:, 3 * chans :]) + 0.5
    new_memory = forget * memory + ingate * candidate
    return outgate * jnp.tanh(new_memory), new_memory


def kernel(layers, sectors, *refs):
    for layer in range(layers):
        pl.when(lax.axis_index("layer") == layer)(lambda layer=layer: layer_program(layer, layers, sectors, *refs))


def layer_program(
    layer, layers, sectors,
    frames, weights, biases, hidden_init, cell_init, h_out, cell_out,
    w, bias, stage_h, stage_c, stage_u, u_far, h_old, h_new, hs, uc, us, cell_old, cell_edge, cell_mid, cell_new,
    partial_mid, partial_near, partial_rim, partial_side, load_sem, edge_send, edge_recv, next_send, next_recv, late_sem,
):
    sector = lax.axis_index("lon")
    right, left = lax.rem(sector + 1, sectors), lax.rem(sector + sectors - 1, sectors)
    steps, rows, cols, chans = stage_u.shape
    base, top = layer == 0, layer == layers - 1
    first, last = sector == 0, sector == sectors - 1
    far_right = jnp.logical_or(sector == sectors // 2 - 1, last)
    far_left = jnp.logical_or(sector == sectors // 2, first)
    far = jnp.logical_or(far_right, far_left)
    slow = jnp.logical_or(sector == sectors // 2 - 1, sector == sectors // 2)
    far_or_last = jnp.logical_and(far, jnp.logical_not(first))
    flipped = lax.rem(sector, 4) == 3
    h_at = [h_old] + [h_new.at[t] for t in range(steps)]
    cell_at = [cell_old, cell_mid, cell_new]
    partial = {"mid": partial_mid, "near": partial_near, "rim": partial_rim, "side": partial_side, "other": partial_side}
    at_start, after = [], {}
    if not base:
        at_start = [(0, "mid"), (0, "near"), (0, "rim")]
        after = {(0, "mid"): (1, "mid"), (0, "rim"): (1, "near")}
        if layer > 1:
            at_start.append((0, "side"))
        if layer == 2:
            after[1, "mid"] = (1, "rim")
    ahead = [*at_start, *after.values()] + ([(0, "other")] if layer == 1 else [])

    load_h = pltpu.make_async_copy(hidden_init.at[0], stage_h, load_sem.at[0])
    load_c = pltpu.make_async_copy(cell_init.at[0], stage_c, load_sem.at[1])
    load_u = [pltpu.make_async_copy(frames.at[t], stage_u.at[t], load_sem.at[2 + t]) for t in range(steps)]
    load_b = pltpu.make_async_copy(biases, bias, load_sem.at[4])
    load_w = [pltpu.make_async_copy(weights.at[0, i], w.at[i], load_sem.at[5]) for i in range(9)]

    barrier = pltpu.get_barrier_semaphore()
    load_h.start()
    load_c.start()
    if base:
        load_u[0].start()
    pl.semaphore_signal(barrier, inc=1, device_id=(layer, left), device_id_type=MESH)

    @pl.when(jnp.logical_not(last))
    def _():
        pl.semaphore_signal(barrier, inc=1, device_id=(layer, right), device_id_type=MESH)

    if not base:
        pl.semaphore_signal(barrier, inc=1, device_id=(layer - 1, sector), device_id_type=MESH)
    else:
        @pl.when(far)
        def _():
            pl.semaphore_signal(barrier, inc=1, device_id=(layers - 1, sectors - 1 - sector), device_id_type=MESH)

    if top:

        @pl.when(far)
        def _():
            for copy in load_u:
                copy.start()

    for copy in load_w:
        copy.start()
    load_b.start()
    if base:
        load_u[1].start()

    def wait_columns(sem, count):
        pair = hs.at[0, :, pl.ds(0, count // 2)] if count % 2 == 0 else hs.at[0, 0, pl.ds(0, count)]
        pltpu.make_async_copy(pair, pair, sem).wait()

    def edge_copies(index, buffer, width):
        return [
            pltpu.make_async_remote_copy(
                src_ref=buffer.at[pl.ds(source, width)],
                dst_ref=buffer.at[pl.ds(target, width)],
                send_sem=edge_send,
                recv_sem=edge_recv.at[2 * index + which],
                device_id=(layer, side),
                device_id_type=MESH,
            )
            for side, source, target, which in (
                (right, PAD + cols - width, PAD - width, 0),
                (left, PAD, PAD + cols, 1),
            )
        ]

    width = EDGE - layer
    edges_h = edge_copies(0, h_old, width)
    edges_c = edge_copies(2, cell_edge, width - 1)
    edges_u = [edge_copies(t, uc.at[t], width - t) for t in range(steps)] if base else []
    soon = [edges_h, edges_c]

    def place(target, staged, start, stop):
        target[pl.ds(PAD + start, stop - start)] = jnp.swapaxes(staged[:, start:stop], 0, 1)

    def shift_into(center, shifted, start, count):
        above, below = row_shifts(center[pl.ds(start, count)])
        shifted[0, pl.ds(start, count)] = above
        shifted[1, pl.ds(start, count)] = below

    def start_edges(groups):
        for edges in groups:
            edges[0].start()

        @pl.when(jnp.logical_not(first))
        def _():
            for edges in groups:
                edges[1].start()

    def start_inputs(t):
        pl.when(jnp.logical_not(far_right))(edges_u[t][0].start)
        pl.when(jnp.logical_not(far_left))(edges_u[t][1].start)

    def start_edges_late():
        pl.semaphore_wait(late_sem, 1)
        for edges in soon:
            edges[1].start()

    def start_far_inputs():
        for copy in load_u:
            copy.wait()
        for which, chosen, source in ((0, far_right, cols - 8), (1, far_left, 0)):

            @pl.when(chosen)
            def _():
                for t in range(steps):
                    u_far[t] = jnp.swapaxes(stage_u[t, :, source : source + 8], 0, 1)
                for t in range(steps):
                    count = EDGE - t
                    pltpu.make_async_remote_copy(
                        src_ref=u_far.at[t, pl.ds((8 - count, 0)[which], count)],
                        dst_ref=uc.at[t, pl.ds((PAD - count, PAD + cols)[which], count)],
                        send_sem=edge_send,
                        recv_sem=edge_recv.at[2 * t + which],
                        device_id=(0, sectors - 1 - sector),
                        device_id_type=MESH,
                    ).start()

    def greet():
        awaited = 3 - first.astype(jnp.int32)
        if top:
            awaited = awaited - 1 + far.astype(jnp.int32)
        pl.semaphore_wait(barrier, awaited)

    @pl.when(last)
    def _():
        greet()
        pl.semaphore_signal(late_sem, inc=1, device_id=(layer, right), device_id_type=MESH)
        if top:
            start_far_inputs()

    load_h.wait()
    place(h_old, stage_h, 0, cols)
    if base:
        pl.when(last)(lambda: start_edges([edges_h]))
    load_c.wait()
    place(cell_old, stage_c, 0, cols)
    for start in (PAD, PAD + cols - EDGE + 1):
        cell_edge[pl.ds(start, EDGE - 1)] = cell_old[pl.ds(start, EDGE - 1)].astype(jnp.bfloat16)
    if base:
        pl.when(last)(lambda: start_edges([edges_c]))
        load_u[0].wait()
        place(uc.at[0], stage_u.at[0], 0, cols)
        pl.when(last)(lambda: start_inputs(0))
        shift_into(uc.at[0], us.at[0], PAD, cols)
    shift_into(h_old, hs.at[0], PAD, cols)

    def finish_edges(which):
        wait_columns(edge_recv.at[which], 2 * width if base else width)
        start = (PAD - width, PAD + cols)[which]
        shift_into(h_old, hs.at[0], start, width)
        if base:
            shift_into(uc.at[0], us.at[0], start, width)

    def finish_cells(which):
        wait_columns(edge_recv.at[4 + which], width - 1)
        edge = pl.ds((PAD - width + 1, PAD + cols)[which], width - 1)
        cell_old[edge] = cell_edge[edge].astype(jnp.float32)

    def finish_second_input(which):
        wait_columns(edge_recv.at[2 + which], width - 1)
        shift_into(uc.at[1], us.at[1], (PAD - EDGE + 1, PAD + cols)[which], EDGE - 1)

    def is_left(chunk):
        return flipped if chunk == "side" else jnp.logical_not(flipped)

    def on_side(chunk, act):
        pl.when(is_left(chunk))(lambda: act(0))
        pl.when(jnp.logical_not(is_left(chunk)))(lambda: act(1))

    def spans(depth, chunk):
        if chunk == "mid":
            return (PAD + 10 + depth,), 12 - 2 * depth
        if chunk == "near":
            return (PAD + 5 + depth, PAD + 22 - depth), 5
        if chunk == "rim":
            return (PAD + 1 + depth, PAD + 27 - depth), 4
        return (jnp.where(is_left(chunk), PAD - 4 + depth, PAD + 31 - depth),), 5

    def to_next(t, chunk, source):
        starts, count = spans(source + t, chunk)
        return [
            (
                pltpu.make_async_remote_copy(
                    src_ref=h_new.at[t, pl.ds(start, count)],
                    dst_ref=uc.at[t, pl.ds(start, count)],
                    send_sem=next_send,
                    recv_sem=next_recv.at[t, CHUNKS.index(chunk)],
                    device_id=(source + 1, sector),
                    device_id_type=MESH,
                ),
                start,
                count,
            )
            for start in starts
        ]

    def windows(center, shifted, starts, count):
        pick = (lambda s: shifted[0, s], lambda s: center[s], lambda s: shifted[1, s])
        return [
            jnp.concatenate([pick[a](pl.ds(start + b - 1, count)).reshape(-1, chans) for start in starts], axis=0)
            for a in range(3)
            for b in range(3)
        ]

    def product(parts, filters):
        return jnp.dot(
            jnp.concatenate(parts, axis=1), filters.reshape(-1, 4 * chans), preferred_element_type=jnp.float32
        )

    def prepare(t, chunk):
        starts, count = spans(layer + t, chunk)
        sums = product(windows(h_at[t], hs.at[t], starts, count), w[:, chans:]) + bias[...]
        partial[chunk][pl.ds(0, sums.shape[0])] = sums

    def compute(t, chunk):
        starts, count = spans(layer + t, chunk)
        inputs = windows(uc.at[t], us.at[t], starts, count)
        if (t, chunk) in ahead:
            sums = product(inputs, w[:, :chans])
            sums = sums + partial[chunk][pl.ds(0, sums.shape[0])]
        else:
            pairs = zip(inputs, windows(h_at[t], hs.at[t], starts, count))
            sums = product([part for pair in pairs for part in pair], w[...]) + bias[...]
        if t == 0 and chunk in ("side", "other"):
            on_side(chunk, finish_cells)
        memory = jnp.concatenate([cell_at[t][pl.ds(start, count)].reshape(-1, chans) for start in starts], axis=0)
        hidden, memory = gate_update(sums, memory)
        hidden = hidden.astype(jnp.bfloat16).reshape(len(starts), count, rows, chans)
        memory = memory.reshape(len(starts), count, rows, chans)
        for i, start in enumerate(starts):
            h_new[t, pl.ds(start, count)] = hidden[i]
            cell_at[t + 1][pl.ds(start, count)] = memory[i]
        if t + 1 < steps:
            for i, start in enumerate(starts):
                above, below = row_shifts(hidden[i])
                hs[t + 1, 0, pl.ds(start, count)] = above
                hs[t + 1, 1, pl.ds(start, count)] = below

    def write_columns(t, start, stop):
        h_out[t, :, start:stop] = jnp.swapaxes(h_new[t, PAD + start : PAD + stop], 0, 1)
        if t == steps - 1:
            cell_out[:, start:stop] = jnp.swapaxes(cell_new[PAD + start : PAD + stop], 0, 1)

    pltpu.make_async_copy(weights.at[0], w, load_sem.at[5]).wait()
    load_b.wait()
    if not base:
        for t, chunk in at_start:
            if chunk != "side":
                prepare(t, chunk)
        pl.when(jnp.logical_not(last))(greet)
        if layer == 1:
            pl.when(far_or_last)(lambda: start_edges(soon))
        else:
            start_edges(soon)
        if top:
            pl.when(jnp.logical_and(far, jnp.logical_not(last)))(start_far_inputs)
        if (0, "side") in ahead:
            on_side("side", finish_edges)
            prepare(0, "side")

    for t, chunk in ORDER:
        if (t, chunk) == (0, "side"):
            if base:
                pl.when(first)(start_edges_late)
            if (0, "side") not in ahead:
                on_side("side", finish_edges)
        if (t, chunk) == (0, "other"):
            on_side("other", finish_edges)
            if (0, "other") in ahead:
                prepare(0, "other")
        if base and t == 1 and chunk in ("side", "other"):
            on_side(chunk, finish_second_input)
        if base:
            if (t, chunk) == (0, "near"):
                load_u[1].wait()
        else:
            arrivals = to_next(t, chunk, layer - 1)
            wait_columns(next_recv.at[t, CHUNKS.index(chunk)], sum(count for _, _, count in arrivals))
            for _, start, count in arrivals:
                shift_into(uc.at[t], us.at[t], start, count)
        compute(t, chunk)
        if base and (t, chunk) == (0, "near"):
            place(uc.at[1], stage_u.at[1], 0, cols)
            shift_into(uc.at[1], us.at[1], PAD, cols)
        if base and chunk in ("mid", "near") and t == 0:
            now = slow if chunk == "near" else jnp.logical_not(slow)

            @pl.when(now)
            def _():
                pl.when(jnp.logical_not(last))(greet)
                for copy, _, _ in to_next(0, "mid", layer):
                    copy.start()

                @pl.when(jnp.logical_not(last))
                def _():
                    start_edges([edges_h])
                    start_inputs(0)
                    start_edges([edges_c])

        if not top and not (base and (t, chunk) == (0, "mid")):
            for copy, _, _ in to_next(t, chunk, layer):
                copy.start()
        if base and (t, chunk) == (0, "near"):
            start_inputs(1)
        if layer == 1 and (t, chunk) == (0, "mid"):
            pl.when(jnp.logical_not(far_or_last))(lambda: start_edges(soon))
        if (t, chunk) in after:
            prepare(*after[t, chunk])
        if not base and (t, chunk) == (1, "mid"):
            pl.when(first)(start_edges_late)

    for t in range(steps):
        write_columns(t, 0, cols)

    sent = 2 * (2 * width - 1)
    inputs = 2 * EDGE - 1
    if base:
        pl.when(far)(lambda: wait_columns(edge_send, sent + inputs))
        pl.when(jnp.logical_not(far))(lambda: wait_columns(edge_send, sent + 2 * inputs))
    elif top:
        pl.when(far)(lambda: wait_columns(edge_send, sent + inputs))
        pl.when(jnp.logical_not(far))(lambda: wait_columns(edge_send, sent))
    else:
        wait_columns(edge_send, sent)
    if not top:
        wait_columns(next_send, sum(piece[2] for t, chunk in ORDER for piece in to_next(t, chunk, layer)))


def finish(h_ref, cell_ref, hidden_out, cell_out, sems):
    copies = [
        pltpu.make_async_copy(h_ref, hidden_out.at[0], sems.at[0]),
        pltpu.make_async_copy(cell_ref, cell_out.at[0], sems.at[1]),
    ]
    for copy in copies:
        copy.start()
    for copy in copies:
        copy.wait()


def solution(mesh):
    layers, sectors = mesh.shape["layer"], mesh.shape["lon"]

    def local(frames, weights, biases, hidden_init, cell_init):
        steps, rows, cols, chans = frames.shape
        bf16, f32 = jnp.bfloat16, jnp.float32
        in_hbm = pl.BlockSpec(memory_space=pltpu.HBM)
        in_vmem = pl.BlockSpec(memory_space=pltpu.VMEM)
        operands = [
            pltpu.with_memory_space_constraint(x, pltpu.HBM)
            for x in (frames, weights, biases, hidden_init, cell_init)
        ]
        hidden, memory = pl.pallas_call(
            lambda *refs: kernel(layers, sectors, *refs),
            out_shape=[
                pltpu.VMEM((steps, rows, cols, chans), bf16),
                pltpu.VMEM((rows, cols, chans), f32),
            ],
            in_specs=[in_hbm] * 5,
            out_specs=[in_vmem] * 2,
            scratch_shapes=[
                pltpu.VMEM((9, 2 * chans, 4 * chans), bf16),
                pltpu.VMEM((1, 4 * chans), f32),
                pltpu.VMEM((rows, cols, chans), bf16),
                pltpu.VMEM((rows, cols, chans), f32),
                pltpu.VMEM((steps, rows, cols, chans), bf16),
                pltpu.VMEM((steps, 8, rows, chans), bf16),
                pltpu.VMEM((WIDTH, rows, chans), bf16),
                pltpu.VMEM((steps, WIDTH, rows, chans), bf16),
                pltpu.VMEM((steps, 2, WIDTH, rows, chans), bf16),
                pltpu.VMEM((steps, WIDTH, rows, chans), bf16),
                pltpu.VMEM((steps, 2, WIDTH, rows, chans), bf16),
                pltpu.VMEM((WIDTH, rows, chans), f32),
                pltpu.VMEM((WIDTH, rows, chans), bf16),
                pltpu.VMEM((WIDTH, rows, chans), f32),
                pltpu.VMEM((WIDTH, rows, chans), f32),
                pltpu.VMEM((12 * rows, 4 * chans), f32),
                pltpu.VMEM((10 * rows, 4 * chans), f32),
                pltpu.VMEM((8 * rows, 4 * chans), f32),
                pltpu.VMEM((5 * rows, 4 * chans), f32),
                pltpu.SemaphoreType.DMA((6,)),
                pltpu.SemaphoreType.DMA,
                pltpu.SemaphoreType.DMA((6,)),
                pltpu.SemaphoreType.DMA,
                pltpu.SemaphoreType.DMA((steps, 5)),
                pltpu.SemaphoreType.REGULAR,
            ],
            compiler_params=pltpu.CompilerParams(
                collective_id=0, has_side_effects=True, vmem_limit_bytes=40 * 1024 * 1024
            ),
            name="conv_lstm",
        )(*operands)
        hidden = pltpu.with_memory_space_constraint(hidden, pltpu.VMEM)
        memory = pltpu.with_memory_space_constraint(memory, pltpu.VMEM)
        return pl.pallas_call(
            finish,
            out_shape=[
                jax.ShapeDtypeStruct((1, steps, rows, cols, chans), bf16),
                jax.ShapeDtypeStruct((1, rows, cols, chans), f32),
            ],
            in_specs=[in_vmem] * 2,
            out_specs=[in_hbm] * 2,
            scratch_shapes=[pltpu.SemaphoreType.DMA((2,))],
            compiler_params=pltpu.CompilerParams(vmem_limit_bytes=16 * 1024 * 1024),
            name="write_out",
        )(hidden, memory)

    in_specs = (
        P(None, None, "lon", None),
        P("layer", None, None, None),
        P("layer", None),
        P("layer", None, "lon", None),
        P("layer", None, "lon", None),
    )
    out_specs = (P("layer", None, None, "lon", None), P("layer", None, "lon", None))
    return jax.shard_map(local, mesh=mesh, in_specs=in_specs, out_specs=out_specs, check_vma=False)
```

```python
import jax
import jax.numpy as jnp
from jax import lax
from jax.experimental import pallas as pl
from jax.experimental.pallas import tpu as pltpu
from jax.sharding import PartitionSpec as P

MESH = pl.DeviceIdType.MESH
PAD = 8
WIDTH = 48
EDGE = 5
BLOCKS = (
    ((0, "mid"),), ((0, "near"),), ((1, "mid"),), ((1, "near"),), ((0, "side"),), ((1, "side"),), ((0, "other"),), ((1, "other"),),
)
CHUNKS = ("mid", "near", "side", "other")


def row_shifts(columns):
    blank = jnp.zeros((columns.shape[0], 1, columns.shape[2]), columns.dtype)
    above = jnp.concatenate([blank, columns[:, :-1]], axis=1)
    below = jnp.concatenate([columns[:, 1:], blank], axis=1)
    return above, below


def gate_update(gate_sums, memory):
    chans = memory.shape[-1]
    ingate = 0.5 * jnp.tanh(0.5 * gate_sums[:, :chans]) + 0.5
    forget = 0.5 * jnp.tanh(0.5 * gate_sums[:, chans : 2 * chans]) + 0.5
    candidate = jnp.tanh(gate_sums[:, 2 * chans : 3 * chans])
    outgate = 0.5 * jnp.tanh(0.5 * gate_sums[:, 3 * chans :]) + 0.5
    new_memory = forget * memory + ingate * candidate
    return outgate * jnp.tanh(new_memory), new_memory


def kernel(layers, sectors, *refs):
    for layer in range(layers):
        pl.when(lax.axis_index("layer") == layer)(lambda layer=layer: layer_program(layer, layers, sectors, *refs))


def layer_program(
    layer, layers, sectors,
    frames, weights, biases, hidden_init, cell_init, h_out, cell_out,
    w, bias, stage_h, stage_c, stage_u, u_far, h_old, h_new, hs, uc, us, cell_old, cell_edge, cell_mid, cell_new,
    partial_mid, partial_near, partial_side, load_sem, edge_send, edge_recv, next_send, next_recv, late_sem,
):
    sector = lax.axis_index("lon")
    right, left = lax.rem(sector + 1, sectors), lax.rem(sector + sectors - 1, sectors)
    steps, rows, cols, chans = stage_u.shape
    base, top = layer == 0, layer == layers - 1
    first, last = sector == 0, sector == sectors - 1
    far_right = jnp.logical_or(sector == sectors // 2 - 1, last)
    far_left = jnp.logical_or(sector == sectors // 2, first)
    far = jnp.logical_or(far_right, far_left)
    far_or_last = jnp.logical_and(far, jnp.logical_not(first))
    flipped = lax.rem(sector, 4) == 3
    h_at = [h_old] + [h_new.at[t] for t in range(steps)]
    cell_at = [cell_old, cell_mid, cell_new]
    partial = {"mid": partial_mid, "near": partial_near, "side": partial_side, "other": partial_side}
    ahead = [] if base else [(0, "mid"), (0, "near"), (1, "near")]
    if layer > 1:
        ahead += [(1, "mid"), (0, "side")]

    load_h = pltpu.make_async_copy(hidden_init.at[0], stage_h, load_sem.at[0])
    load_c = pltpu.make_async_copy(cell_init.at[0], stage_c, load_sem.at[1])
    load_u = [pltpu.make_async_copy(frames.at[t], stage_u.at[t], load_sem.at[2 + t]) for t in range(steps)]
    load_b = pltpu.make_async_copy(biases, bias, load_sem.at[4])
    load_w = [pltpu.make_async_copy(weights.at[0, i], w.at[i], load_sem.at[5]) for i in range(9)]

    barrier = pltpu.get_barrier_semaphore()

    @pl.when(jnp.logical_not(last))
    def _():
        pl.semaphore_signal(barrier, inc=1, device_id=(layer, right), device_id_type=MESH)

    pl.semaphore_signal(barrier, inc=1, device_id=(layer, left), device_id_type=MESH)
    load_h.start()
    load_c.start()
    if not base:
        pl.semaphore_signal(barrier, inc=1, device_id=(layer - 1, sector), device_id_type=MESH)
    else:
        @pl.when(far)
        def _():
            pl.semaphore_signal(barrier, inc=1, device_id=(layers - 1, sectors - 1 - sector), device_id_type=MESH)

    def load_rest():
        if base:
            load_u[0].start()
        if top:

            @pl.when(far)
            def _():
                for copy in load_u:
                    copy.start()

        for copy in load_w:
            copy.start()
        load_b.start()
        if base:
            load_u[1].start()

    if base:
        pl.when(jnp.logical_not(last))(load_rest)
    else:
        load_rest()

    def wait_columns(sem, count):
        pair = hs.at[0, :, pl.ds(0, count // 2)] if count % 2 == 0 else hs.at[0, 0, pl.ds(0, count)]
        pltpu.make_async_copy(pair, pair, sem).wait()

    def edge_copies(index, buffer, width):
        return [
            pltpu.make_async_remote_copy(
                src_ref=buffer.at[pl.ds(source, width)],
                dst_ref=buffer.at[pl.ds(target, width)],
                send_sem=edge_send,
                recv_sem=edge_recv.at[2 * index + which],
                device_id=(layer, side),
                device_id_type=MESH,
            )
            for side, source, target, which in (
                (right, PAD + cols - width, PAD - width, 0),
                (left, PAD, PAD + cols, 1),
            )
        ]

    width = EDGE - layer
    edges_h = edge_copies(0, h_old, width)
    edges_c = edge_copies(2, cell_edge, width - 1)
    edges_u = [edge_copies(t, uc.at[t], width - t) for t in range(steps)] if base else []
    soon = [edges_h, edges_c]

    def place(target, staged, start, stop):
        target[pl.ds(PAD + start, stop - start)] = jnp.swapaxes(staged[:, start:stop], 0, 1)

    def shift_into(center, shifted, start, count):
        above, below = row_shifts(center[pl.ds(start, count)])
        shifted[0, pl.ds(start, count)] = above
        shifted[1, pl.ds(start, count)] = below

    def start_edges(groups):
        for edges in groups:
            edges[0].start()

        @pl.when(jnp.logical_not(first))
        def _():
            for edges in groups:
                edges[1].start()

    def start_inputs(t):
        pl.when(jnp.logical_not(far_right))(edges_u[t][0].start)
        pl.when(jnp.logical_not(far_left))(edges_u[t][1].start)

    def start_edges_late():
        pl.semaphore_wait(late_sem, 1)
        for edges in soon:
            edges[1].start()

    def start_far_inputs():
        for copy in load_u:
            copy.wait()
        for which, chosen, source in ((0, far_right, cols - 8), (1, far_left, 0)):

            @pl.when(chosen)
            def _():
                for t in range(steps):
                    u_far[t] = jnp.swapaxes(stage_u[t, :, source : source + 8], 0, 1)
                for t in range(steps):
                    count = EDGE - t
                    pltpu.make_async_remote_copy(
                        src_ref=u_far.at[t, pl.ds((8 - count, 0)[which], count)],
                        dst_ref=uc.at[t, pl.ds((PAD - count, PAD + cols)[which], count)],
                        send_sem=edge_send,
                        recv_sem=edge_recv.at[2 * t + which],
                        device_id=(0, sectors - 1 - sector),
                        device_id_type=MESH,
                    ).start()

    def greet():
        awaited = 3 - first.astype(jnp.int32)
        if top:
            awaited = awaited - 1 + far.astype(jnp.int32)
        pl.semaphore_wait(barrier, awaited)

    @pl.when(last)
    def _():
        greet()
        pl.semaphore_signal(late_sem, inc=1, device_id=(layer, right), device_id_type=MESH)
        if top:
            start_far_inputs()

    load_h.wait()
    place(h_old, stage_h, 0, cols)
    if base:
        pl.when(last)(lambda: start_edges([edges_h]))
    load_c.wait()
    if base:
        pl.when(last)(load_rest)
    place(cell_old, stage_c, 0, cols)
    for start in (PAD, PAD + cols - EDGE + 1):
        cell_edge[pl.ds(start, EDGE - 1)] = cell_old[pl.ds(start, EDGE - 1)].astype(jnp.bfloat16)
    if base:
        pl.when(last)(lambda: start_edges([edges_c]))
        load_u[0].wait()
        place(uc.at[0], stage_u.at[0], 0, cols)
        pl.when(last)(lambda: start_inputs(0))
        shift_into(uc.at[0], us.at[0], PAD, cols)
    shift_into(h_old, hs.at[0], PAD, cols)

    def finish_edges(which):
        wait_columns(edge_recv.at[which], 2 * width if base else width)
        start = (PAD - width, PAD + cols)[which]
        shift_into(h_old, hs.at[0], start, width)
        if base:
            shift_into(uc.at[0], us.at[0], start, width)

    def finish_cells(which):
        wait_columns(edge_recv.at[4 + which], width - 1)
        edge = pl.ds((PAD - width + 1, PAD + cols)[which], width - 1)
        cell_old[edge] = cell_edge[edge].astype(jnp.float32)

    def finish_second_input(which):
        wait_columns(edge_recv.at[2 + which], width - 1)
        shift_into(uc.at[1], us.at[1], (PAD - EDGE + 1, PAD + cols)[which], EDGE - 1)

    def is_left(chunk):
        return flipped if chunk == "side" else jnp.logical_not(flipped)

    def on_side(chunk, act):
        pl.when(is_left(chunk))(lambda: act(0))
        pl.when(jnp.logical_not(is_left(chunk)))(lambda: act(1))

    def spans(depth, chunk):
        if chunk == "mid":
            return (PAD + 8 + depth,), 16 - 2 * depth
        if chunk == "near":
            return (PAD + 1 + depth, PAD + 24 - depth), 7
        return (jnp.where(is_left(chunk), PAD - 4 + depth, PAD + 31 - depth),), 5

    def to_next(t, chunk, source, half=None):
        starts, count = spans(source + t, chunk)
        if half is not None:
            count //= 2
            starts = (starts[0] + half * count,)
        return [
            (
                pltpu.make_async_remote_copy(
                    src_ref=h_new.at[t, pl.ds(start, count)],
                    dst_ref=uc.at[t, pl.ds(start, count)],
                    send_sem=next_send,
                    recv_sem=next_recv.at[t, CHUNKS.index(chunk)],
                    device_id=(source + 1, sector),
                    device_id_type=MESH,
                ),
                start,
                count,
            )
            for start in starts
        ]

    def windows(center, shifted, starts, count):
        pick = (lambda s: shifted[0, s], lambda s: center[s], lambda s: shifted[1, s])
        return [
            jnp.concatenate([pick[a](pl.ds(start + b - 1, count)).reshape(-1, chans) for start in starts], axis=0)
            for a in range(3)
            for b in range(3)
        ]

    def product(parts, filters):
        return jnp.dot(
            jnp.concatenate(parts, axis=1), filters.reshape(-1, 4 * chans), preferred_element_type=jnp.float32
        )

    def prepare(t, chunk):
        starts, count = spans(layer + t, chunk)
        sums = product(windows(h_at[t], hs.at[t], starts, count), w[:, chans:]) + bias[...]
        partial[chunk][pl.ds(0, sums.shape[0])] = sums

    def compute(t, chunk, half=None):
        starts, count = spans(layer + t, chunk)
        rows_of = pl.ds(0, len(starts) * count * rows)
        if half is not None:
            count //= 2
            starts = (starts[0] + half * count,)
            rows_of = pl.ds(half * count * rows, count * rows)
        inputs = windows(uc.at[t], us.at[t], starts, count)
        if (t, chunk) in ahead:
            sums = product(inputs, w[:, :chans])
            sums = sums + partial[chunk][rows_of]
        else:
            pairs = zip(inputs, windows(h_at[t], hs.at[t], starts, count))
            sums = product([part for pair in pairs for part in pair], w[...]) + bias[...]
        if t == 0 and chunk in ("side", "other"):
            on_side(chunk, finish_cells)
        memory = jnp.concatenate([cell_at[t][pl.ds(start, count)].reshape(-1, chans) for start in starts], axis=0)
        hidden, memory = gate_update(sums, memory)
        hidden = hidden.astype(jnp.bfloat16).reshape(len(starts), count, rows, chans)
        memory = memory.reshape(len(starts), count, rows, chans)
        for i, start in enumerate(starts):
            h_new[t, pl.ds(start, count)] = hidden[i]
            cell_at[t + 1][pl.ds(start, count)] = memory[i]
        if t + 1 < steps:
            for i, start in enumerate(starts):
                above, below = row_shifts(hidden[i])
                hs[t + 1, 0, pl.ds(start, count)] = above
                hs[t + 1, 1, pl.ds(start, count)] = below

    def write_columns(t, start, stop):
        h_out[t, :, start:stop] = jnp.swapaxes(h_new[t, PAD + start : PAD + stop], 0, 1)
        if t == steps - 1:
            cell_out[:, start:stop] = jnp.swapaxes(cell_new[PAD + start : PAD + stop], 0, 1)

    pltpu.make_async_copy(weights.at[0], w, load_sem.at[5]).wait()
    load_b.wait()
    if not base:
        prepare(0, "mid")
        prepare(0, "near")
        pl.when(jnp.logical_not(last))(greet)
        if layer == 1:
            pl.when(far_or_last)(lambda: start_edges(soon))
        else:
            start_edges(soon)
        if top:
            pl.when(jnp.logical_and(far, jnp.logical_not(last)))(start_far_inputs)
        if (0, "side") in ahead:
            on_side("side", finish_edges)
            prepare(0, "side")

    for block in BLOCKS:
        if (0, "side") in block:
            if base:
                pl.when(first)(start_edges_late)
            if (0, "side") not in ahead:
                on_side("side", finish_edges)
        if (0, "other") in block:
            on_side("other", finish_edges)
            if (0, "other") in ahead:
                prepare(0, "other")
        if (1, "side") in block and base:
            on_side("side", finish_second_input)
        if (1, "other") in block and base:
            on_side("other", finish_second_input)
        if base:
            if block == BLOCKS[1]:
                load_u[1].wait()
        else:
            arrivals = [(t, chunk, *piece) for t, chunk in block for piece in to_next(t, chunk, layer - 1)]
            for t, chunk in block:
                wait_columns(next_recv.at[t, CHUNKS.index(chunk)], sum(a[4] for a in arrivals if a[:2] == (t, chunk)))
            for t, _, _, start, count in arrivals:
                shift_into(uc.at[t], us.at[t], start, count)
        halved = layer == 1 and block == BLOCKS[0]
        for t, chunk in block:
            if halved:
                for half in range(2):
                    compute(t, chunk, half)
                    to_next(t, chunk, layer, half)[0][0].start()
            else:
                if top and (t, chunk) == (1, "other"):
                    write_columns(0, 0, cols)
                    write_columns(1, 8, cols - 8)
                compute(t, chunk)
        if base and block == BLOCKS[0]:

            pl.when(jnp.logical_not(last))(greet)

        if base and block == BLOCKS[1]:
            place(uc.at[1], stage_u.at[1], 0, cols)
            shift_into(uc.at[1], us.at[1], PAD, cols)
        if not top and not halved:
            for t, chunk in block:
                for copy, _, _ in to_next(t, chunk, layer):
                    copy.start()
        if base and block == BLOCKS[0]:

            @pl.when(jnp.logical_not(last))
            def _():
                start_edges([edges_h])
                start_inputs(0)
                start_edges([edges_c])

        if base and block == BLOCKS[1]:
            start_inputs(1)
        if not base:
            if block == BLOCKS[0]:
                if layer == 1:
                    pl.when(jnp.logical_not(far_or_last))(lambda: start_edges(soon))
                if (1, "mid") in ahead:
                    prepare(1, "mid")
            if block == BLOCKS[1]:
                prepare(1, "near")
            if block == BLOCKS[2]:
                pl.when(first)(start_edges_late)

    if top:
        write_columns(1, 0, 8)
        write_columns(1, cols - 8, cols)
    else:
        for t in range(steps):
            write_columns(t, 0, cols)

    sent = 2 * (2 * width - 1)
    inputs = 2 * EDGE - 1
    if base:
        pl.when(far)(lambda: wait_columns(edge_send, sent + inputs))
        pl.when(jnp.logical_not(far))(lambda: wait_columns(edge_send, sent + 2 * inputs))
    elif top:
        pl.when(far)(lambda: wait_columns(edge_send, sent + inputs))
        pl.when(jnp.logical_not(far))(lambda: wait_columns(edge_send, sent))
    else:
        wait_columns(edge_send, sent)
    if not top:
        wait_columns(next_send, sum(piece[2] for block in BLOCKS for t, chunk in block for piece in to_next(t, chunk, layer)))


def finish(h_ref, cell_ref, hidden_out, cell_out, sems):
    copies = [
        pltpu.make_async_copy(h_ref, hidden_out.at[0], sems.at[0]),
        pltpu.make_async_copy(cell_ref, cell_out.at[0], sems.at[1]),
    ]
    for copy in copies:
        copy.start()
    for copy in copies:
        copy.wait()


def solution(mesh):
    layers, sectors = mesh.shape["layer"], mesh.shape["lon"]

    def local(frames, weights, biases, hidden_init, cell_init):
        steps, rows, cols, chans = frames.shape
        bf16, f32 = jnp.bfloat16, jnp.float32
        in_hbm = pl.BlockSpec(memory_space=pltpu.HBM)
        in_vmem = pl.BlockSpec(memory_space=pltpu.VMEM)
        operands = [
            pltpu.with_memory_space_constraint(x, pltpu.HBM)
            for x in (frames, weights, biases, hidden_init, cell_init)
        ]
        hidden, memory = pl.pallas_call(
            lambda *refs: kernel(layers, sectors, *refs),
            out_shape=[
                pltpu.VMEM((steps, rows, cols, chans), bf16),
                pltpu.VMEM((rows, cols, chans), f32),
            ],
            in_specs=[in_hbm] * 5,
            out_specs=[in_vmem] * 2,
            scratch_shapes=[
                pltpu.VMEM((9, 2 * chans, 4 * chans), bf16),
                pltpu.VMEM((1, 4 * chans), f32),
                pltpu.VMEM((rows, cols, chans), bf16),
                pltpu.VMEM((rows, cols, chans), f32),
                pltpu.VMEM((steps, rows, cols, chans), bf16),
                pltpu.VMEM((steps, 8, rows, chans), bf16),
                pltpu.VMEM((WIDTH, rows, chans), bf16),
                pltpu.VMEM((steps, WIDTH, rows, chans), bf16),
                pltpu.VMEM((steps, 2, WIDTH, rows, chans), bf16),
                pltpu.VMEM((steps, WIDTH, rows, chans), bf16),
                pltpu.VMEM((steps, 2, WIDTH, rows, chans), bf16),
                pltpu.VMEM((WIDTH, rows, chans), f32),
                pltpu.VMEM((WIDTH, rows, chans), bf16),
                pltpu.VMEM((WIDTH, rows, chans), f32),
                pltpu.VMEM((WIDTH, rows, chans), f32),
                pltpu.VMEM((16 * rows, 4 * chans), f32),
                pltpu.VMEM((14 * rows, 4 * chans), f32),
                pltpu.VMEM((5 * rows, 4 * chans), f32),
                pltpu.SemaphoreType.DMA((6,)),
                pltpu.SemaphoreType.DMA,
                pltpu.SemaphoreType.DMA((6,)),
                pltpu.SemaphoreType.DMA,
                pltpu.SemaphoreType.DMA((steps, 4)),
                pltpu.SemaphoreType.REGULAR,
            ],
            compiler_params=pltpu.CompilerParams(
                collective_id=0, has_side_effects=True, vmem_limit_bytes=40 * 1024 * 1024
            ),
            name="conv_lstm",
        )(*operands)
        hidden = pltpu.with_memory_space_constraint(hidden, pltpu.VMEM)
        memory = pltpu.with_memory_space_constraint(memory, pltpu.VMEM)
        return pl.pallas_call(
            finish,
            out_shape=[
                jax.ShapeDtypeStruct((1, steps, rows, cols, chans), bf16),
                jax.ShapeDtypeStruct((1, rows, cols, chans), f32),
            ],
            in_specs=[in_vmem] * 2,
            out_specs=[in_hbm] * 2,
            scratch_shapes=[pltpu.SemaphoreType.DMA((2,))],
            compiler_params=pltpu.CompilerParams(vmem_limit_bytes=16 * 1024 * 1024),
            name="write_out",
        )(hidden, memory)

    in_specs = (
        P(None, None, "lon", None),
        P("layer", None, None, None),
        P("layer", None),
        P("layer", None, "lon", None),
        P("layer", None, "lon", None),
    )
    out_specs = (P("layer", None, None, "lon", None), P("layer", None, "lon", None))
    return jax.shard_map(local, mesh=mesh, in_specs=in_specs, out_specs=out_specs, check_vma=False)
```

```python
import jax
import jax.numpy as jnp
from jax import lax
from jax.experimental import pallas as pl
from jax.experimental.pallas import tpu as pltpu
from jax.sharding import PartitionSpec as P

MESH = pl.DeviceIdType.MESH
PAD = 8
WIDTH = 48
EDGE = 5
BLOCKS = (
    ((0, "mid"),), ((0, "near"),), ((1, "mid"),), ((1, "near"),), ((0, "side"),), ((1, "side"),), ((0, "other"),), ((1, "other"),),
)
CHUNKS = ("mid", "near", "side", "other")


def row_shifts(columns):
    blank = jnp.zeros((columns.shape[0], 1, columns.shape[2]), columns.dtype)
    above = jnp.concatenate([blank, columns[:, :-1]], axis=1)
    below = jnp.concatenate([columns[:, 1:], blank], axis=1)
    return above, below


def gate_update(gate_sums, memory):
    chans = memory.shape[-1]
    ingate = 0.5 * jnp.tanh(0.5 * gate_sums[:, :chans]) + 0.5
    forget = 0.5 * jnp.tanh(0.5 * gate_sums[:, chans : 2 * chans]) + 0.5
    candidate = jnp.tanh(gate_sums[:, 2 * chans : 3 * chans])
    outgate = 0.5 * jnp.tanh(0.5 * gate_sums[:, 3 * chans :]) + 0.5
    new_memory = forget * memory + ingate * candidate
    return outgate * jnp.tanh(new_memory), new_memory


def kernel(layers, sectors, *refs):
    for layer in range(layers):
        pl.when(lax.axis_index("layer") == layer)(lambda layer=layer: layer_program(layer, layers, sectors, *refs))


def layer_program(
    layer, layers, sectors,
    frames, weights, biases, hidden_init, cell_init, h_out, cell_out,
    w, bias, stage_h, stage_c, stage_u, u_far, h_old, h_new, hs, uc, us, cell_old, cell_edge, cell_mid, cell_new,
    partial_mid, partial_near, partial_side, load_sem, edge_send, edge_recv, next_send, next_recv, late_sem,
):
    sector = lax.axis_index("lon")
    right, left = lax.rem(sector + 1, sectors), lax.rem(sector + sectors - 1, sectors)
    steps, rows, cols, chans = stage_u.shape
    base, top = layer == 0, layer == layers - 1
    first, last = sector == 0, sector == sectors - 1
    far_right = jnp.logical_or(sector == sectors // 2 - 1, last)
    far_left = jnp.logical_or(sector == sectors // 2, first)
    far = jnp.logical_or(far_right, far_left)
    far_or_last = jnp.logical_and(far, jnp.logical_not(first))
    flipped = lax.rem(sector, 4) == 3
    h_at = [h_old] + [h_new.at[t] for t in range(steps)]
    cell_at = [cell_old, cell_mid, cell_new]
    partial = {"mid": partial_mid, "near": partial_near, "side": partial_side, "other": partial_side}
    ahead = [] if base else [(0, "mid"), (0, "near"), (1, "near")]
    if layer > 1:
        ahead += [(1, "mid"), (0, "side")]
    if layer == 1:
        ahead.append((0, "other"))

    load_h = pltpu.make_async_copy(hidden_init.at[0], stage_h, load_sem.at[0])
    load_c = pltpu.make_async_copy(cell_init.at[0], stage_c, load_sem.at[1])
    load_u = [pltpu.make_async_copy(frames.at[t], stage_u.at[t], load_sem.at[2 + t]) for t in range(steps)]
    load_b = pltpu.make_async_copy(biases, bias, load_sem.at[4])
    load_w = [pltpu.make_async_copy(weights.at[0, i], w.at[i], load_sem.at[5]) for i in range(9)]

    barrier = pltpu.get_barrier_semaphore()

    @pl.when(jnp.logical_not(last))
    def _():
        pl.semaphore_signal(barrier, inc=1, device_id=(layer, right), device_id_type=MESH)

    pl.semaphore_signal(barrier, inc=1, device_id=(layer, left), device_id_type=MESH)
    load_h.start()
    load_c.start()
    if not base:
        pl.semaphore_signal(barrier, inc=1, device_id=(layer - 1, sector), device_id_type=MESH)
    else:
        @pl.when(far)
        def _():
            pl.semaphore_signal(barrier, inc=1, device_id=(layers - 1, sectors - 1 - sector), device_id_type=MESH)

    def load_rest():
        if base:
            load_u[0].start()
        if top:

            @pl.when(far)
            def _():
                for copy in load_u:
                    copy.start()

        for copy in load_w:
            copy.start()
        load_b.start()
        if base:
            load_u[1].start()

    if base:
        pl.when(jnp.logical_not(last))(load_rest)
    else:
        load_rest()

    def wait_columns(sem, count):
        pair = hs.at[0, :, pl.ds(0, count // 2)] if count % 2 == 0 else hs.at[0, 0, pl.ds(0, count)]
        pltpu.make_async_copy(pair, pair, sem).wait()

    def edge_copies(index, buffer, width):
        return [
            pltpu.make_async_remote_copy(
                src_ref=buffer.at[pl.ds(source, width)],
                dst_ref=buffer.at[pl.ds(target, width)],
                send_sem=edge_send,
                recv_sem=edge_recv.at[2 * index + which],
                device_id=(layer, side),
                device_id_type=MESH,
            )
            for side, source, target, which in (
                (right, PAD + cols - width, PAD - width, 0),
                (left, PAD, PAD + cols, 1),
            )
        ]

    width = EDGE - layer
    edges_h = edge_copies(0, h_old, width)
    edges_c = edge_copies(2, cell_edge, width - 1)
    edges_u = [edge_copies(t, uc.at[t], width - t) for t in range(steps)] if base else []
    soon = [edges_h, edges_c]

    def place(target, staged, start, stop):
        target[pl.ds(PAD + start, stop - start)] = jnp.swapaxes(staged[:, start:stop], 0, 1)

    def shift_into(center, shifted, start, count):
        above, below = row_shifts(center[pl.ds(start, count)])
        shifted[0, pl.ds(start, count)] = above
        shifted[1, pl.ds(start, count)] = below

    def start_edges(groups):
        for edges in groups:
            edges[0].start()

        @pl.when(jnp.logical_not(first))
        def _():
            for edges in groups:
                edges[1].start()

    def start_inputs(t):
        pl.when(jnp.logical_not(far_right))(edges_u[t][0].start)
        pl.when(jnp.logical_not(far_left))(edges_u[t][1].start)

    def start_edges_late():
        pl.semaphore_wait(late_sem, 1)
        for edges in soon:
            edges[1].start()

    def start_far_inputs():
        for copy in load_u:
            copy.wait()
        for which, chosen, source in ((0, far_right, cols - 16), (1, far_left, 0)):

            @pl.when(chosen)
            def _():
                for t in range(steps):
                    u_far[t] = jnp.swapaxes(stage_u[t, :, source : source + 16], 0, 1)
                for t in range(steps):
                    count = EDGE - t
                    pltpu.make_async_remote_copy(
                        src_ref=u_far.at[t, pl.ds((16 - count, 0)[which], count)],
                        dst_ref=uc.at[t, pl.ds((PAD - count, PAD + cols)[which], count)],
                        send_sem=edge_send,
                        recv_sem=edge_recv.at[2 * t + which],
                        device_id=(0, sectors - 1 - sector),
                        device_id_type=MESH,
                    ).start()

    def greet():
        awaited = 3 - first.astype(jnp.int32)
        if top:
            awaited = awaited - 1 + far.astype(jnp.int32)
        pl.semaphore_wait(barrier, awaited)

    @pl.when(last)
    def _():
        greet()
        pl.semaphore_signal(late_sem, inc=1, device_id=(layer, right), device_id_type=MESH)
        if top:
            start_far_inputs()

    load_h.wait()
    place(h_old, stage_h, 0, cols)
    if base:
        pl.when(last)(lambda: start_edges([edges_h]))
    load_c.wait()
    if base:
        pl.when(last)(load_rest)
    place(cell_old, stage_c, 0, cols)
    for start in (PAD, PAD + cols - EDGE + 1):
        cell_edge[pl.ds(start, EDGE - 1)] = cell_old[pl.ds(start, EDGE - 1)].astype(jnp.bfloat16)
    if base:
        pl.when(last)(lambda: start_edges([edges_c]))
        load_u[0].wait()
        place(uc.at[0], stage_u.at[0], 0, cols)
        pl.when(last)(lambda: start_inputs(0))
        shift_into(uc.at[0], us.at[0], PAD, cols)
    shift_into(h_old, hs.at[0], PAD, cols)

    def finish_edges(which):
        wait_columns(edge_recv.at[which], 2 * width if base else width)
        start = (PAD - width, PAD + cols)[which]
        shift_into(h_old, hs.at[0], start, width)
        if base:
            shift_into(uc.at[0], us.at[0], start, width)

    def finish_cells(which):
        wait_columns(edge_recv.at[4 + which], width - 1)
        edge = pl.ds((PAD - width + 1, PAD + cols)[which], width - 1)
        cell_old[edge] = cell_edge[edge].astype(jnp.float32)

    def finish_second_input(which):
        wait_columns(edge_recv.at[2 + which], width - 1)
        shift_into(uc.at[1], us.at[1], (PAD - EDGE + 1, PAD + cols)[which], EDGE - 1)

    def is_left(chunk):
        return flipped if chunk == "side" else jnp.logical_not(flipped)

    def on_side(chunk, act):
        pl.when(is_left(chunk))(lambda: act(0))
        pl.when(jnp.logical_not(is_left(chunk)))(lambda: act(1))

    def spans(depth, chunk):
        if chunk == "mid":
            return (PAD + 8 + depth,), 16 - 2 * depth
        if chunk == "near":
            return (PAD + 1 + depth, PAD + 24 - depth), 7
        return (jnp.where(is_left(chunk), PAD - 4 + depth, PAD + 31 - depth),), 5

    def to_next(t, chunk, source, half=None):
        starts, count = spans(source + t, chunk)
        if half is not None:
            count //= 2
            starts = (starts[0] + half * count,)
        return [
            (
                pltpu.make_async_remote_copy(
                    src_ref=h_new.at[t, pl.ds(start, count)],
                    dst_ref=uc.at[t, pl.ds(start, count)],
                    send_sem=next_send,
                    recv_sem=next_recv.at[t, CHUNKS.index(chunk)],
                    device_id=(source + 1, sector),
                    device_id_type=MESH,
                ),
                start,
                count,
            )
            for start in starts
        ]

    def windows(center, shifted, starts, count):
        pick = (lambda s: shifted[0, s], lambda s: center[s], lambda s: shifted[1, s])
        return [
            jnp.concatenate([pick[a](pl.ds(start + b - 1, count)).reshape(-1, chans) for start in starts], axis=0)
            for a in range(3)
            for b in range(3)
        ]

    def product(parts, filters):
        return jnp.dot(
            jnp.concatenate(parts, axis=1), filters.reshape(-1, 4 * chans), preferred_element_type=jnp.float32
        )

    def prepare(t, chunk):
        starts, count = spans(layer + t, chunk)
        sums = product(windows(h_at[t], hs.at[t], starts, count), w[:, chans:]) + bias[...]
        partial[chunk][pl.ds(0, sums.shape[0])] = sums

    def compute(t, chunk, half=None):
        starts, count = spans(layer + t, chunk)
        rows_of = pl.ds(0, len(starts) * count * rows)
        if half is not None:
            count //= 2
            starts = (starts[0] + half * count,)
            rows_of = pl.ds(half * count * rows, count * rows)
        inputs = windows(uc.at[t], us.at[t], starts, count)
        if (t, chunk) in ahead:
            sums = product(inputs, w[:, :chans])
            sums = sums + partial[chunk][rows_of]
        else:
            pairs = zip(inputs, windows(h_at[t], hs.at[t], starts, count))
            sums = product([part for pair in pairs for part in pair], w[...]) + bias[...]
        if t == 0 and chunk in ("side", "other"):
            on_side(chunk, finish_cells)
        memory = jnp.concatenate([cell_at[t][pl.ds(start, count)].reshape(-1, chans) for start in starts], axis=0)
        hidden, memory = gate_update(sums, memory)
        hidden = hidden.astype(jnp.bfloat16).reshape(len(starts), count, rows, chans)
        memory = memory.reshape(len(starts), count, rows, chans)
        for i, start in enumerate(starts):
            h_new[t, pl.ds(start, count)] = hidden[i]
            cell_at[t + 1][pl.ds(start, count)] = memory[i]
        if t + 1 < steps:
            for i, start in enumerate(starts):
                above, below = row_shifts(hidden[i])
                hs[t + 1, 0, pl.ds(start, count)] = above
                hs[t + 1, 1, pl.ds(start, count)] = below

    def write_columns(t):
        h_out[t] = jnp.swapaxes(h_new[t, PAD : PAD + cols], 0, 1)
        if t == steps - 1:
            cell_out[...] = jnp.swapaxes(cell_new[PAD : PAD + cols], 0, 1)

    pltpu.make_async_copy(weights.at[0], w, load_sem.at[5]).wait()
    load_b.wait()
    if not base:
        prepare(0, "mid")
        prepare(0, "near")
        pl.when(jnp.logical_not(last))(greet)
        if layer == 1:
            pl.when(far_or_last)(lambda: start_edges(soon))
        else:
            start_edges(soon)
        if top:
            pl.when(jnp.logical_and(far, jnp.logical_not(last)))(start_far_inputs)
        if (0, "side") in ahead:
            on_side("side", finish_edges)
            prepare(0, "side")

    for block in BLOCKS:
        if (0, "side") in block:
            if base:
                pl.when(first)(start_edges_late)
            if (0, "side") not in ahead:
                on_side("side", finish_edges)
        if (0, "other") in block:
            on_side("other", finish_edges)
            if (0, "other") in ahead:
                prepare(0, "other")
        if (1, "side") in block and base:
            on_side("side", finish_second_input)
        if (1, "other") in block and base:
            on_side("other", finish_second_input)
        if base:
            if block == BLOCKS[1]:
                load_u[1].wait()
        else:
            arrivals = [(t, chunk, *piece) for t, chunk in block for piece in to_next(t, chunk, layer - 1)]
            for t, chunk in block:
                wait_columns(next_recv.at[t, CHUNKS.index(chunk)], sum(a[4] for a in arrivals if a[:2] == (t, chunk)))
            for t, _, _, start, count in arrivals:
                shift_into(uc.at[t], us.at[t], start, count)
        halved = layer == 1 and block == BLOCKS[0]
        for t, chunk in block:
            if halved:
                for half in range(2):
                    compute(t, chunk, half)
                    to_next(t, chunk, layer, half)[0][0].start()
            else:
                compute(t, chunk)
        if base and block == BLOCKS[0]:

            pl.when(jnp.logical_not(last))(greet)

        if base and block == BLOCKS[1]:
            place(uc.at[1], stage_u.at[1], 0, cols)
            shift_into(uc.at[1], us.at[1], PAD, cols)
        if not top and not halved:
            for t, chunk in block:
                for copy, _, _ in to_next(t, chunk, layer):
                    copy.start()
        if base and block == BLOCKS[0]:

            @pl.when(jnp.logical_not(last))
            def _():
                start_edges([edges_h])
                start_inputs(0)
                start_edges([edges_c])

        if base and block == BLOCKS[1]:
            start_inputs(1)
        if not base:
            if block == BLOCKS[0]:
                if layer == 1:
                    pl.when(jnp.logical_not(far_or_last))(lambda: start_edges(soon))
                if (1, "mid") in ahead:
                    prepare(1, "mid")
            if block == BLOCKS[1]:
                prepare(1, "near")
            if block == BLOCKS[2]:
                pl.when(first)(start_edges_late)

    for t in range(steps):
        write_columns(t)

    sent = 2 * (2 * width - 1)
    inputs = 2 * EDGE - 1
    if base:
        pl.when(far)(lambda: wait_columns(edge_send, sent + inputs))
        pl.when(jnp.logical_not(far))(lambda: wait_columns(edge_send, sent + 2 * inputs))
    elif top:
        pl.when(far)(lambda: wait_columns(edge_send, sent + inputs))
        pl.when(jnp.logical_not(far))(lambda: wait_columns(edge_send, sent))
    else:
        wait_columns(edge_send, sent)
    if not top:
        wait_columns(next_send, sum(piece[2] for block in BLOCKS for t, chunk in block for piece in to_next(t, chunk, layer)))


def finish(h_ref, cell_ref, hidden_out, cell_out, sems):
    copies = [
        pltpu.make_async_copy(h_ref, hidden_out.at[0], sems.at[0]),
        pltpu.make_async_copy(cell_ref, cell_out.at[0], sems.at[1]),
    ]
    for copy in copies:
        copy.start()
    for copy in copies:
        copy.wait()


def solution(mesh):
    layers, sectors = mesh.shape["layer"], mesh.shape["lon"]

    def local(frames, weights, biases, hidden_init, cell_init):
        steps, rows, cols, chans = frames.shape
        bf16, f32 = jnp.bfloat16, jnp.float32
        in_hbm = pl.BlockSpec(memory_space=pltpu.HBM)
        in_vmem = pl.BlockSpec(memory_space=pltpu.VMEM)
        operands = [
            pltpu.with_memory_space_constraint(x, pltpu.HBM)
            for x in (frames, weights, biases, hidden_init, cell_init)
        ]
        hidden, memory = pl.pallas_call(
            lambda *refs: kernel(layers, sectors, *refs),
            out_shape=[
                pltpu.VMEM((steps, rows, cols, chans), bf16),
                pltpu.VMEM((rows, cols, chans), f32),
            ],
            in_specs=[in_hbm] * 5,
            out_specs=[in_vmem] * 2,
            scratch_shapes=[
                pltpu.VMEM((9, 2 * chans, 4 * chans), bf16),
                pltpu.VMEM((1, 4 * chans), f32),
                pltpu.VMEM((rows, cols, chans), bf16),
                pltpu.VMEM((rows, cols, chans), f32),
                pltpu.VMEM((steps, rows, cols, chans), bf16),
                pltpu.VMEM((steps, 16, rows, chans), bf16),
                pltpu.VMEM((WIDTH, rows, chans), bf16),
                pltpu.VMEM((steps, WIDTH, rows, chans), bf16),
                pltpu.VMEM((steps, 2, WIDTH, rows, chans), bf16),
                pltpu.VMEM((steps, WIDTH, rows, chans), bf16),
                pltpu.VMEM((steps, 2, WIDTH, rows, chans), bf16),
                pltpu.VMEM((WIDTH, rows, chans), f32),
                pltpu.VMEM((WIDTH, rows, chans), bf16),
                pltpu.VMEM((WIDTH, rows, chans), f32),
                pltpu.VMEM((WIDTH, rows, chans), f32),
                pltpu.VMEM((16 * rows, 4 * chans), f32),
                pltpu.VMEM((14 * rows, 4 * chans), f32),
                pltpu.VMEM((5 * rows, 4 * chans), f32),
                pltpu.SemaphoreType.DMA((6,)),
                pltpu.SemaphoreType.DMA,
                pltpu.SemaphoreType.DMA((6,)),
                pltpu.SemaphoreType.DMA,
                pltpu.SemaphoreType.DMA((steps, 4)),
                pltpu.SemaphoreType.REGULAR,
            ],
            compiler_params=pltpu.CompilerParams(
                collective_id=0, has_side_effects=True, vmem_limit_bytes=40 * 1024 * 1024
            ),
            name="conv_lstm",
        )(*operands)
        hidden = pltpu.with_memory_space_constraint(hidden, pltpu.VMEM)
        memory = pltpu.with_memory_space_constraint(memory, pltpu.VMEM)
        return pl.pallas_call(
            finish,
            out_shape=[
                jax.ShapeDtypeStruct((1, steps, rows, cols, chans), bf16),
                jax.ShapeDtypeStruct((1, rows, cols, chans), f32),
            ],
            in_specs=[in_vmem] * 2,
            out_specs=[in_hbm] * 2,
            scratch_shapes=[pltpu.SemaphoreType.DMA((2,))],
            compiler_params=pltpu.CompilerParams(vmem_limit_bytes=16 * 1024 * 1024),
            name="write_out",
        )(hidden, memory)

    in_specs = (
        P(None, None, "lon", None),
        P("layer", None, None, None),
        P("layer", None),
        P("layer", None, "lon", None),
        P("layer", None, "lon", None),
    )
    out_specs = (P("layer", None, None, "lon", None), P("layer", None, "lon", None))
    return jax.shard_map(local, mesh=mesh, in_specs=in_specs, out_specs=out_specs, check_vma=False)
```

```python
import jax
import jax.numpy as jnp
from jax import lax
from jax.experimental import pallas as pl
from jax.experimental.pallas import tpu as pltpu
from jax.sharding import PartitionSpec as P

MESH = pl.DeviceIdType.MESH
PAD = 8
WIDTH = 48
EDGE = 5
BLOCKS = (
    ((0, "mid"),), ((0, "near"),), ((1, "mid"),), ((1, "near"),), ((0, "side"),), ((1, "side"),), ((0, "other"),), ((1, "other"),),
)
CHUNKS = ("mid", "near", "side", "other")


def row_shifts(columns):
    blank = jnp.zeros((columns.shape[0], 1, columns.shape[2]), columns.dtype)
    above = jnp.concatenate([blank, columns[:, :-1]], axis=1)
    below = jnp.concatenate([columns[:, 1:], blank], axis=1)
    return above, below


def gate_update(gate_sums, memory):
    chans = memory.shape[-1]
    ingate = 0.5 * jnp.tanh(0.5 * gate_sums[:, :chans]) + 0.5
    forget = 0.5 * jnp.tanh(0.5 * gate_sums[:, chans : 2 * chans]) + 0.5
    candidate = jnp.tanh(gate_sums[:, 2 * chans : 3 * chans])
    outgate = 0.5 * jnp.tanh(0.5 * gate_sums[:, 3 * chans :]) + 0.5
    new_memory = forget * memory + ingate * candidate
    return outgate * jnp.tanh(new_memory), new_memory


def kernel(layers, sectors, *refs):
    for layer in range(layers):
        pl.when(lax.axis_index("layer") == layer)(lambda layer=layer: layer_program(layer, layers, sectors, *refs))


def layer_program(
    layer, layers, sectors,
    frames, weights, biases, hidden_init, cell_init, h_out, cell_out,
    w, bias, stage_h, stage_c, stage_u, u_far, h_old, h_new, hs, uc, us, cell_old, cell_edge, cell_mid, cell_new,
    partial_mid, partial_near, partial_side, load_sem, edge_send, edge_recv, next_send, next_recv, late_sem,
):
    sector = lax.axis_index("lon")
    right, left = lax.rem(sector + 1, sectors), lax.rem(sector + sectors - 1, sectors)
    steps, rows, cols, chans = stage_u.shape
    base, top = layer == 0, layer == layers - 1
    first, last = sector == 0, sector == sectors - 1
    far_right = jnp.logical_or(sector == sectors // 2 - 1, last)
    far_left = jnp.logical_or(sector == sectors // 2, first)
    far = jnp.logical_or(far_right, far_left)
    far_or_last = jnp.logical_and(far, jnp.logical_not(first))
    flipped = lax.rem(sector, 4) == 3
    h_at = [h_old] + [h_new.at[t] for t in range(steps)]
    cell_at = [cell_old, cell_mid, cell_new]
    partial = {"mid": partial_mid, "near": partial_near, "side": partial_side, "other": partial_side}
    ahead = [] if base else [(0, "mid"), (0, "near"), (1, "near")]
    if layer > 1:
        ahead += [(1, "mid"), (0, "side")]
    if layer in (1, 2):
        ahead.append((0, "other"))

    load_h = pltpu.make_async_copy(hidden_init.at[0], stage_h, load_sem.at[0])
    load_c = pltpu.make_async_copy(cell_init.at[0], stage_c, load_sem.at[1])
    load_u = [pltpu.make_async_copy(frames.at[t], stage_u.at[t], load_sem.at[2 + t]) for t in range(steps)]
    load_b = pltpu.make_async_copy(biases, bias, load_sem.at[4])
    load_w = [pltpu.make_async_copy(weights.at[0, i], w.at[i], load_sem.at[5]) for i in range(9)]

    barrier = pltpu.get_barrier_semaphore()

    @pl.when(jnp.logical_not(last))
    def _():
        pl.semaphore_signal(barrier, inc=1, device_id=(layer, right), device_id_type=MESH)

    pl.semaphore_signal(barrier, inc=1, device_id=(layer, left), device_id_type=MESH)
    load_h.start()
    load_c.start()
    if not base:
        pl.semaphore_signal(barrier, inc=1, device_id=(layer - 1, sector), device_id_type=MESH)
    else:
        @pl.when(far)
        def _():
            pl.semaphore_signal(barrier, inc=1, device_id=(layers - 1, sectors - 1 - sector), device_id_type=MESH)

    def load_rest():
        if base:
            load_u[0].start()
        if top:

            @pl.when(far)
            def _():
                for copy in load_u:
                    copy.start()

        for copy in load_w:
            copy.start()
        load_b.start()
        if base:
            load_u[1].start()

    if base:
        pl.when(jnp.logical_not(last))(load_rest)
    else:
        load_rest()

    def wait_columns(sem, count):
        pair = hs.at[0, :, pl.ds(0, count // 2)] if count % 2 == 0 else hs.at[0, 0, pl.ds(0, count)]
        pltpu.make_async_copy(pair, pair, sem).wait()

    def edge_copies(index, buffer, width):
        return [
            pltpu.make_async_remote_copy(
                src_ref=buffer.at[pl.ds(source, width)],
                dst_ref=buffer.at[pl.ds(target, width)],
                send_sem=edge_send,
                recv_sem=edge_recv.at[2 * index + which],
                device_id=(layer, side),
                device_id_type=MESH,
            )
            for side, source, target, which in (
                (right, PAD + cols - width, PAD - width, 0),
                (left, PAD, PAD + cols, 1),
            )
        ]

    width = EDGE - layer
    edges_h = edge_copies(0, h_old, width)
    edges_c = edge_copies(2, cell_edge, width - 1)
    edges_u = [edge_copies(t, uc.at[t], width - t) for t in range(steps)] if base else []
    soon = [edges_h, edges_c]

    def place(target, staged, start, stop):
        target[pl.ds(PAD + start, stop - start)] = jnp.swapaxes(staged[:, start:stop], 0, 1)

    def shift_into(center, shifted, start, count):
        above, below = row_shifts(center[pl.ds(start, count)])
        shifted[0, pl.ds(start, count)] = above
        shifted[1, pl.ds(start, count)] = below

    def start_edges(groups):
        for edges in groups:
            edges[0].start()

        @pl.when(jnp.logical_not(first))
        def _():
            for edges in groups:
                edges[1].start()

    def start_inputs(t):
        pl.when(jnp.logical_not(far_right))(edges_u[t][0].start)
        pl.when(jnp.logical_not(far_left))(edges_u[t][1].start)

    def start_edges_late():
        pl.semaphore_wait(late_sem, 1)
        for edges in soon:
            edges[1].start()

    def start_far_inputs():
        for copy in load_u:
            copy.wait()
        for which, chosen, source in ((0, far_right, cols - 16), (1, far_left, 0)):

            @pl.when(chosen)
            def _():
                for t in range(steps):
                    u_far[t] = jnp.swapaxes(stage_u[t, :, source : source + 16], 0, 1)
                for t in range(steps):
                    count = EDGE - t
                    pltpu.make_async_remote_copy(
                        src_ref=u_far.at[t, pl.ds((16 - count, 0)[which], count)],
                        dst_ref=uc.at[t, pl.ds((PAD - count, PAD + cols)[which], count)],
                        send_sem=edge_send,
                        recv_sem=edge_recv.at[2 * t + which],
                        device_id=(0, sectors - 1 - sector),
                        device_id_type=MESH,
                    ).start()

    def greet():
        awaited = 3 - first.astype(jnp.int32)
        if top:
            awaited = awaited - 1 + far.astype(jnp.int32)
        pl.semaphore_wait(barrier, awaited)

    @pl.when(last)
    def _():
        greet()
        pl.semaphore_signal(late_sem, inc=1, device_id=(layer, right), device_id_type=MESH)
        if top:
            start_far_inputs()

    load_h.wait()
    place(h_old, stage_h, 0, cols)
    if base:
        pl.when(last)(lambda: start_edges([edges_h]))
    load_c.wait()
    if base:
        pl.when(last)(load_rest)
    place(cell_old, stage_c, 0, cols)
    for start in (PAD, PAD + cols - EDGE + 1):
        cell_edge[pl.ds(start, EDGE - 1)] = cell_old[pl.ds(start, EDGE - 1)].astype(jnp.bfloat16)
    if base:
        pl.when(last)(lambda: start_edges([edges_c]))
        load_u[0].wait()
        place(uc.at[0], stage_u.at[0], 0, cols)
        pl.when(last)(lambda: start_inputs(0))
        shift_into(uc.at[0], us.at[0], PAD, cols)
    shift_into(h_old, hs.at[0], PAD, cols)

    def finish_edges(which):
        wait_columns(edge_recv.at[which], 2 * width if base else width)
        start = (PAD - width, PAD + cols)[which]
        shift_into(h_old, hs.at[0], start, width)
        if base:
            shift_into(uc.at[0], us.at[0], start, width)

    def finish_cells(which):
        wait_columns(edge_recv.at[4 + which], width - 1)
        edge = pl.ds((PAD - width + 1, PAD + cols)[which], width - 1)
        cell_old[edge] = cell_edge[edge].astype(jnp.float32)

    def finish_second_input(which):
        wait_columns(edge_recv.at[2 + which], width - 1)
        shift_into(uc.at[1], us.at[1], (PAD - EDGE + 1, PAD + cols)[which], EDGE - 1)

    def is_left(chunk):
        return flipped if chunk == "side" else jnp.logical_not(flipped)

    def on_side(chunk, act):
        pl.when(is_left(chunk))(lambda: act(0))
        pl.when(jnp.logical_not(is_left(chunk)))(lambda: act(1))

    def spans(depth, chunk):
        if chunk == "mid":
            return (PAD + 8 + depth,), 16 - 2 * depth
        if chunk == "near":
            return (PAD + 1 + depth, PAD + 24 - depth), 7
        return (jnp.where(is_left(chunk), PAD - 4 + depth, PAD + 31 - depth),), 5

    def to_next(t, chunk, source, half=None):
        starts, count = spans(source + t, chunk)
        if half is not None:
            count //= 2
            starts = (starts[0] + half * count,)
        return [
            (
                pltpu.make_async_remote_copy(
                    src_ref=h_new.at[t, pl.ds(start, count)],
                    dst_ref=uc.at[t, pl.ds(start, count)],
                    send_sem=next_send,
                    recv_sem=next_recv.at[t, CHUNKS.index(chunk)],
                    device_id=(source + 1, sector),
                    device_id_type=MESH,
                ),
                start,
                count,
            )
            for start in starts
        ]

    def windows(center, shifted, starts, count):
        pick = (lambda s: shifted[0, s], lambda s: center[s], lambda s: shifted[1, s])
        return [
            jnp.concatenate([pick[a](pl.ds(start + b - 1, count)).reshape(-1, chans) for start in starts], axis=0)
            for a in range(3)
            for b in range(3)
        ]

    def product(parts, filters):
        return jnp.dot(
            jnp.concatenate(parts, axis=1), filters.reshape(-1, 4 * chans), preferred_element_type=jnp.float32
        )

    def prepare(t, chunk):
        starts, count = spans(layer + t, chunk)
        sums = product(windows(h_at[t], hs.at[t], starts, count), w[:, chans:]) + bias[...]
        partial[chunk][pl.ds(0, sums.shape[0])] = sums

    def compute(t, chunk, half=None):
        starts, count = spans(layer + t, chunk)
        rows_of = pl.ds(0, len(starts) * count * rows)
        if half is not None:
            count //= 2
            starts = (starts[0] + half * count,)
            rows_of = pl.ds(half * count * rows, count * rows)
        inputs = windows(uc.at[t], us.at[t], starts, count)
        if (t, chunk) in ahead:
            sums = product(inputs, w[:, :chans])
            sums = sums + partial[chunk][rows_of]
        else:
            pairs = zip(inputs, windows(h_at[t], hs.at[t], starts, count))
            sums = product([part for pair in pairs for part in pair], w[...]) + bias[...]
        if t == 0 and chunk in ("side", "other"):
            on_side(chunk, finish_cells)
        memory = jnp.concatenate([cell_at[t][pl.ds(start, count)].reshape(-1, chans) for start in starts], axis=0)
        hidden, memory = gate_update(sums, memory)
        hidden = hidden.astype(jnp.bfloat16).reshape(len(starts), count, rows, chans)
        memory = memory.reshape(len(starts), count, rows, chans)
        for i, start in enumerate(starts):
            h_new[t, pl.ds(start, count)] = hidden[i]
            cell_at[t + 1][pl.ds(start, count)] = memory[i]
        if t + 1 < steps:
            for i, start in enumerate(starts):
                above, below = row_shifts(hidden[i])
                hs[t + 1, 0, pl.ds(start, count)] = above
                hs[t + 1, 1, pl.ds(start, count)] = below

    def write_columns(t):
        h_out[t] = jnp.swapaxes(h_new[t, PAD : PAD + cols], 0, 1)
        if t == steps - 1:
            cell_out[...] = jnp.swapaxes(cell_new[PAD : PAD + cols], 0, 1)

    pltpu.make_async_copy(weights.at[0], w, load_sem.at[5]).wait()
    load_b.wait()
    if not base:
        prepare(0, "mid")
        prepare(0, "near")
        pl.when(jnp.logical_not(last))(greet)
        if layer == 1:
            pl.when(far_or_last)(lambda: start_edges(soon))
        else:
            start_edges(soon)
        if top:
            pl.when(jnp.logical_and(far, jnp.logical_not(last)))(start_far_inputs)
        if (0, "side") in ahead:
            on_side("side", finish_edges)
            prepare(0, "side")

    for block in BLOCKS:
        if (0, "side") in block:
            if base:
                pl.when(first)(start_edges_late)
            if (0, "side") not in ahead:
                on_side("side", finish_edges)
        if (0, "other") in block:
            on_side("other", finish_edges)
            if (0, "other") in ahead:
                prepare(0, "other")
        if (1, "side") in block and base:
            on_side("side", finish_second_input)
        if (1, "other") in block and base:
            on_side("other", finish_second_input)
        if base:
            if block == BLOCKS[1]:
                load_u[1].wait()
        else:
            arrivals = [(t, chunk, *piece) for t, chunk in block for piece in to_next(t, chunk, layer - 1)]
            for t, chunk in block:
                wait_columns(next_recv.at[t, CHUNKS.index(chunk)], sum(a[4] for a in arrivals if a[:2] == (t, chunk)))
            for t, _, _, start, count in arrivals:
                shift_into(uc.at[t], us.at[t], start, count)
        halved = layer == 1 and block == BLOCKS[0]
        for t, chunk in block:
            if halved:
                for half in range(2):
                    compute(t, chunk, half)
                    to_next(t, chunk, layer, half)[0][0].start()
            else:
                compute(t, chunk)
        if base and block == BLOCKS[0]:

            pl.when(jnp.logical_not(last))(greet)

        if base and block == BLOCKS[1]:
            place(uc.at[1], stage_u.at[1], 0, cols)
            shift_into(uc.at[1], us.at[1], PAD, cols)
        if not top and not halved:
            for t, chunk in block:
                for copy, _, _ in to_next(t, chunk, layer):
                    copy.start()
        if base and block == BLOCKS[0]:

            @pl.when(jnp.logical_not(last))
            def _():
                start_edges([edges_h])
                start_inputs(0)
                start_edges([edges_c])

        if base and block == BLOCKS[1]:
            start_inputs(1)
        if not base:
            if block == BLOCKS[0]:
                if layer == 1:
                    pl.when(jnp.logical_not(far_or_last))(lambda: start_edges(soon))
                if (1, "mid") in ahead:
                    prepare(1, "mid")
            if block == BLOCKS[1]:
                prepare(1, "near")
            if block == BLOCKS[2]:
                pl.when(first)(start_edges_late)

    for t in range(steps):
        write_columns(t)

    sent = 2 * (2 * width - 1)
    inputs = 2 * EDGE - 1
    if base:
        pl.when(far)(lambda: wait_columns(edge_send, sent + inputs))
        pl.when(jnp.logical_not(far))(lambda: wait_columns(edge_send, sent + 2 * inputs))
    elif top:
        pl.when(far)(lambda: wait_columns(edge_send, sent + inputs))
        pl.when(jnp.logical_not(far))(lambda: wait_columns(edge_send, sent))
    else:
        wait_columns(edge_send, sent)
    if not top:
        wait_columns(next_send, sum(piece[2] for block in BLOCKS for t, chunk in block for piece in to_next(t, chunk, layer)))


def finish(h_ref, cell_ref, hidden_out, cell_out, sems):
    copies = [
        pltpu.make_async_copy(h_ref, hidden_out.at[0], sems.at[0]),
        pltpu.make_async_copy(cell_ref, cell_out.at[0], sems.at[1]),
    ]
    for copy in copies:
        copy.start()
    for copy in copies:
        copy.wait()


def solution(mesh):
    layers, sectors = mesh.shape["layer"], mesh.shape["lon"]

    def local(frames, weights, biases, hidden_init, cell_init):
        steps, rows, cols, chans = frames.shape
        bf16, f32 = jnp.bfloat16, jnp.float32
        in_hbm = pl.BlockSpec(memory_space=pltpu.HBM)
        in_vmem = pl.BlockSpec(memory_space=pltpu.VMEM)
        operands = [
            pltpu.with_memory_space_constraint(x, pltpu.HBM)
            for x in (frames, weights, biases, hidden_init, cell_init)
        ]
        hidden, memory = pl.pallas_call(
            lambda *refs: kernel(layers, sectors, *refs),
            out_shape=[
                pltpu.VMEM((steps, rows, cols, chans), bf16),
                pltpu.VMEM((rows, cols, chans), f32),
            ],
            in_specs=[in_hbm] * 5,
            out_specs=[in_vmem] * 2,
            scratch_shapes=[
                pltpu.VMEM((9, 2 * chans, 4 * chans), bf16),
                pltpu.VMEM((1, 4 * chans), f32),
                pltpu.VMEM((rows, cols, chans), bf16),
                pltpu.VMEM((rows, cols, chans), f32),
                pltpu.VMEM((steps, rows, cols, chans), bf16),
                pltpu.VMEM((steps, 16, rows, chans), bf16),
                pltpu.VMEM((WIDTH, rows, chans), bf16),
                pltpu.VMEM((steps, WIDTH, rows, chans), bf16),
                pltpu.VMEM((steps, 2, WIDTH, rows, chans), bf16),
                pltpu.VMEM((steps, WIDTH, rows, chans), bf16),
                pltpu.VMEM((steps, 2, WIDTH, rows, chans), bf16),
                pltpu.VMEM((WIDTH, rows, chans), f32),
                pltpu.VMEM((WIDTH, rows, chans), bf16),
                pltpu.VMEM((WIDTH, rows, chans), f32),
                pltpu.VMEM((WIDTH, rows, chans), f32),
                pltpu.VMEM((16 * rows, 4 * chans), f32),
                pltpu.VMEM((14 * rows, 4 * chans), f32),
                pltpu.VMEM((5 * rows, 4 * chans), f32),
                pltpu.SemaphoreType.DMA((6,)),
                pltpu.SemaphoreType.DMA,
                pltpu.SemaphoreType.DMA((6,)),
                pltpu.SemaphoreType.DMA,
                pltpu.SemaphoreType.DMA((steps, 4)),
                pltpu.SemaphoreType.REGULAR,
            ],
            compiler_params=pltpu.CompilerParams(
                collective_id=0, has_side_effects=True, vmem_limit_bytes=40 * 1024 * 1024
            ),
            name="conv_lstm",
        )(*operands)
        hidden = pltpu.with_memory_space_constraint(hidden, pltpu.VMEM)
        memory = pltpu.with_memory_space_constraint(memory, pltpu.VMEM)
        return pl.pallas_call(
            finish,
            out_shape=[
                jax.ShapeDtypeStruct((1, steps, rows, cols, chans), bf16),
                jax.ShapeDtypeStruct((1, rows, cols, chans), f32),
            ],
            in_specs=[in_vmem] * 2,
            out_specs=[in_hbm] * 2,
            scratch_shapes=[pltpu.SemaphoreType.DMA((2,))],
            compiler_params=pltpu.CompilerParams(vmem_limit_bytes=16 * 1024 * 1024),
            name="write_out",
        )(hidden, memory)

    in_specs = (
        P(None, None, "lon", None),
        P("layer", None, None, None),
        P("layer", None),
        P("layer", None, "lon", None),
        P("layer", None, "lon", None),
    )
    out_specs = (P("layer", None, None, "lon", None), P("layer", None, "lon", None))
    return jax.shard_map(local, mesh=mesh, in_specs=in_specs, out_specs=out_specs, check_vma=False)
```
